256 devices in a mesh: grp: 8 (over x_hi, y), tp: 32 (over x_lo, z, core).
Axes of the slice: x: 4 (x_hi: 2, x_lo: 2; x = x_hi * 2 + x_lo), y: 4, z: 8, core: 2. Of those that a mesh axis runs over, the one named last changes fastest.
Arguments:
- block_tokens: int32 [2560, 4], P('grp'), may hold values from 0 to 15999
- slot_of_row: int32 [2560], P('grp'), may hold values from 0 to 2559, as said below
- cache_lengths: int32 [2560], P('grp'), may hold values from 1 to 4
- embed_table: bfloat16 [16000, 2048], P('tp'), may hold values from -6 to 6
- norm_gain: float32 [8192], replicated, may hold values from 0.1 to 1.9
- query_weight: bfloat16 [8192, 4096], P(None, 'tp'), may hold values from -0.0625 to 0.0625
- key_value_weight: bfloat16 [2, 8192, 4096], P(None, None, 'tp'), may hold values from -0.0625 to 0.0625
- kv_cache: bfloat16 [2, 2560, 4, 4096], P(None, 'grp', None, 'tp'), may hold values from -730 to 730
- out_weight: bfloat16 [4096, 8192], P('tp'), may hold values from -0.1875 to 0.1875
- final_gain: float32 [8192], replicated, may hold values from 0.1 to 1.9
- prefix_weight: bfloat16 [8192, 4096], P(None, 'tp'), may hold values from -0.0625 to 0.0625
Outputs:
- prefix: bfloat16 [2560, 4096], P('grp', 'tp')
The draws below stay inside these ranges and needn't reach their ends.
Inputs may be any that keep to these rules, and one draw needn't show every extreme that they name: `slot_of_row`: A permutation of all slots; slot s belongs to group s // 320. From the rows of one index of grp at most 80 go to one group, and in every draw some index of grp sends exactly 80 to some group.
All inputs are finite; a program needn't handle non-finite values.
Results may differ from the reference program's by a relative error of at most 0.027.
Values may be sent and summed in bfloat16 or wider, within the bound.
A program may use at most 128 MiB of HBM per device.

```python
import math
import jax
import jax.numpy as jnp
import numpy as np
from jax import lax

GW = 8192
BLOCK = 4
TOKW = 2048
HEAD = 128
ATT = 4096
LW = 4096
VOCAB = 16000
CACHE = 4
OWN = 320
ROWS = 2560
N_GRP = 8


def draw_slot_of_row(key, part):
    key = jax.random.fold_in(key, 7)
    keys = jax.random.split(key, 4)
    groups = N_GRP
    base = OWN // groups
    first = jax.random.permutation(keys[0], groups)
    offset = jax.random.randint(keys[1], (), 1, groups)
    second = (first + offset) % groups
    column = jnp.arange(groups, dtype=jnp.int32)
    counts = base + base * (column[None, :] == first[:, None]).astype(jnp.int32) - base * (column[None, :] == second[:, None]).astype(jnp.int32)
    ends = jnp.cumsum(counts, axis=1)
    row_ids = jnp.arange(OWN, dtype=jnp.int32)
    target = jnp.sum((row_ids[None, :, None] >= ends[:, None, :]).astype(jnp.int32), axis=2)
    starts = ends - counts
    within = row_ids[None, :] - jnp.take_along_axis(starts, target, axis=1)
    before = jnp.cumsum(counts, axis=0) - counts
    place = jnp.take_along_axis(before, target, axis=1) + within
    shuffle = jax.vmap(lambda subkey: jax.random.permutation(subkey, OWN))(jax.random.split(keys[2], groups))
    slot_ids = target * OWN + shuffle[target, place]
    order = jax.vmap(lambda subkey: jax.random.permutation(subkey, OWN))(jax.random.split(keys[3], groups))
    slot_ids = jnp.take_along_axis(slot_ids, order, axis=1)
    return slot_ids.reshape(-1).astype(jnp.int32)


def draw_kv_cache(key, part):
    key = jax.random.fold_in(key, 3)
    first = jax.random.fold_in(key, 0)
    values = jnp.clip(jax.random.normal(first, (2, ROWS, CACHE, ATT), jnp.float32), -6.0, 6.0)
    return values.astype(jnp.bfloat16)


def plant(result, stream_key, low, largest):
    longest = result.shape.index(max(result.shape))
    spots = []
    for shift in (0, 1):
        where = [jax.random.randint(jax.random.fold_in(stream_key, axis), (), 0, length) for axis, length in enumerate(result.shape)]
        where[longest] = (where[longest] + shift) % result.shape[longest]
        spots.append(tuple(where))
    return result.at[spots[0]].set(low).at[spots[1]].set(largest)


def spiked(entries, own_key, source, target, shards_of, factor):
    def block_of(axis_at):
        return (jnp.arange(entries.shape[axis_at]) // (entries.shape[axis_at] // shards_of)).reshape((-1,) + (1,) * (entries.ndim - 1 - axis_at))

    first = jax.random.permutation(own_key, shards_of)[block_of(target)]
    second = (block_of(target) + shards_of // 2) % shards_of
    return jnp.where((block_of(source) == first) | (block_of(source) == second), factor * entries, entries)


def block_levels(stream_key, extent, cuts, low, high):
    factor_of = 1.0
    for dim, shards_of in cuts:
        draws = jax.random.uniform(jax.random.fold_in(jax.random.fold_in(stream_key, 6), dim), (shards_of,), jnp.float32, low / len(cuts), high / len(cuts))
        factor_of = factor_of * jnp.repeat(jnp.exp(draws), extent[dim] // shards_of).reshape((-1,) + (1,) * (len(extent) - 1 - dim))
    return factor_of


def cumulative_ranks(number_of, skew):
    loads = [(1 << 20) // math.isqrt(standing ** skew) + 1 for standing in range(1, number_of + 1)]
    scale = 1 + sum(loads) // (1 << 30)
    return np.cumsum(np.array([max(1, weight // scale) for weight in loads]))


def skewed_ids(key, dims, number_of, slope):
    listing = cumulative_ranks(number_of, slope)
    lot = jax.random.randint(jax.random.fold_in(key, 1), dims, 0, int(listing[number_of - 1]))
    standing = jnp.searchsorted(jnp.asarray(listing, jnp.int32), lot, side="right")
    return jax.random.permutation(jax.random.fold_in(key, 2), number_of)[standing].astype(jnp.int32)


def centred(own_key, extent, scale, limit, pieces=(), kind=jnp.bfloat16):
    array = scale * jax.random.normal(own_key, extent, jnp.float32)
    if pieces:
        array = array * block_levels(own_key, extent, pieces, -0.22, 0.18)
    return jnp.clip(array, -limit, limit).astype(kind)


def noise_with(rng, shape, deviation, bound, shards, heavy, kind=jnp.bfloat16):
    values = deviation * jax.random.normal(rng, shape, jnp.float32)
    if shards:
        values = values * block_levels(rng, shape, shards, -0.22, 0.18)
    return jnp.clip(spiked(values, jax.random.fold_in(rng, 3), *heavy), -bound, bound).astype(kind)


def setup_inputs(seed: int = 0) -> dict:
    streams_of = jax.random.split(jax.random.key(seed), 12)
    block_tokens = plant(skewed_ids(streams_of[0], (ROWS, BLOCK), VOCAB, 2), jax.random.fold_in(streams_of[0], 3), 0, VOCAB - 1).astype(jnp.int32)
    slot_of_row = draw_slot_of_row(jax.random.fold_in(streams_of[11], 71), 0)
    cache_lengths = plant(jax.random.randint(streams_of[2], (ROWS,), 1, CACHE + 1), jax.random.fold_in(streams_of[2], 1), 1, CACHE).astype(jnp.int32)
    embed_table = centred(streams_of[3], (VOCAB, TOKW), 1.0, 6.0, ((0, 32),))
    norm_gain = jnp.clip(1.0 + 0.18 * jax.random.normal(streams_of[4], (GW,), jnp.float32), 0.1, 1.9)
    query_weight = centred(streams_of[5], (GW, ATT), GW ** -0.5, 0.0625, ((1, 32),))
    key_value_weight = centred(streams_of[6], (2, GW, ATT), GW ** -0.5, 0.0625, ((2, 32),))
    kv_cache = draw_kv_cache(jax.random.fold_in(streams_of[11], 71), 0)
    out_weight = noise_with(streams_of[8], (ATT, GW), ATT ** -0.5, 0.1875, ((0, 32),), (0, 1, 32, 2.75))
    final_gain = jnp.clip(1.0 + 0.18 * jax.random.normal(streams_of[9], (GW,), jnp.float32), 0.1, 1.9)
    prefix_weight = centred(streams_of[10], (GW, LW), GW ** -0.5, 0.0625, ((1, 32),))
    return {"block_tokens": block_tokens, "slot_of_row": slot_of_row, "cache_lengths": cache_lengths, "embed_table": embed_table, "norm_gain": norm_gain, "query_weight": query_weight, "key_value_weight": key_value_weight, "kv_cache": kv_cache, "out_weight": out_weight, "final_gain": final_gain, "prefix_weight": prefix_weight}


EPSILON = 1e-05

def rms_scale(rows, gain):
    values = rows.astype(jnp.float32)
    spread = lax.optimization_barrier(jnp.mean(values * values, axis=-1, keepdims=True))
    return (values * lax.rsqrt(spread + EPSILON) * gain).astype(jnp.bfloat16)

def reference(block_tokens, slot_of_row, cache_lengths, embed_table, norm_gain, query_weight, key_value_weight, kv_cache, out_weight, final_gain, prefix_weight):
    row_count = block_tokens.shape[0]
    looked = jnp.take(embed_table, block_tokens, axis=0).reshape(row_count, -1)
    ordered = jnp.zeros_like(looked).at[slot_of_row].set(looked)
    normed = rms_scale(ordered, norm_gain)
    queries = jnp.dot(normed, query_weight, preferred_element_type=jnp.float32).astype(jnp.bfloat16)
    fresh_keys = jnp.dot(normed, key_value_weight[0], preferred_element_type=jnp.float32).astype(jnp.bfloat16)
    fresh_values = jnp.dot(normed, key_value_weight[1], preferred_element_type=jnp.float32).astype(jnp.bfloat16)
    heads_all = queries.shape[1] // HEAD
    query_heads = queries.reshape(row_count, heads_all, HEAD).astype(jnp.float32)
    key_heads = fresh_keys.reshape(row_count, heads_all, HEAD).astype(jnp.float32)
    value_heads = fresh_values.reshape(row_count, heads_all, HEAD).astype(jnp.float32)
    cached = kv_cache.reshape(2, row_count, CACHE, heads_all, HEAD)
    scale = 1.0 / HEAD ** 0.5
    past = jnp.einsum('rhd,rchd->rhc', query_heads, cached[0].astype(jnp.float32)) * scale
    valid = jnp.arange(CACHE, dtype=jnp.int32)[None, None, :] < cache_lengths[:, None, None]
    past = jnp.where(valid, past, jnp.float32(-1e+30))
    own_score = lax.optimization_barrier(jnp.sum(query_heads * key_heads, axis=-1))[..., None] * scale
    scores = jnp.concatenate([past, own_score], axis=-1)
    weights = jax.nn.softmax(scores, axis=-1).astype(jnp.bfloat16)
    mixed = jnp.einsum('rhc,rchd->rhd', weights[..., :-1].astype(jnp.float32), cached[1].astype(jnp.float32))
    mixed = mixed + weights[..., -1:].astype(jnp.float32) * value_heads
    attended = mixed.reshape(row_count, -1).astype(jnp.bfloat16)
    projected = jnp.dot(attended, out_weight, preferred_element_type=jnp.float32)
    context = (ordered.astype(jnp.float32) + projected).astype(jnp.bfloat16)
    returned = jnp.take(context, slot_of_row, axis=0)
    final_rows = rms_scale(returned, final_gain)
    return jnp.dot(final_rows, prefix_weight, preferred_element_type=jnp.float32).astype(jnp.bfloat16)
```

```python
import functools

import jax
import jax.numpy as jnp
from jax import lax
from jax.experimental import pallas as pl
from jax.experimental.pallas import tpu as pltpu
from jax.sharding import PartitionSpec as P

MESH = pl.DeviceIdType.MESH
BF = jnp.bfloat16
F32 = jnp.float32
EPSILON = 1e-05
HEAD = 128
CACHE = 4
GROUPS = 8
RING = 8
OWN = 320
HALF = 160
QUART = 80
CAP = 80
LANES = 384
WIDE = 256
CHUNKS = 32
MINE = 16
VOCAB_ROWS = 500
SEMS = 192


def dot(a, b):
    return jnp.dot(a, b, preferred_element_type=F32)


def dot_lanes(a, b):
    return lax.dot_general(a, b, (((1,), (1,)), ((), ())), preferred_element_type=F32)


def ring_order(i):
    step = (i + 1) // 2
    return 4 + step * (1 - 2 * (i % 2))


class Wire:
    def __init__(self, send_sem, recv_sem):
        self.send_sem, self.recv_sem = send_sem, recv_sem
        self.used = 0
        self.sent = []

    def block(self, count):
        first = self.used
        self.used += count
        assert self.used <= SEMS
        return first

    def make(self, src, dst, peer, index):
        return pltpu.make_async_remote_copy(
            src_ref=src,
            dst_ref=dst,
            send_sem=self.send_sem.at[index],
            recv_sem=self.recv_sem.at[index],
            device_id=peer,
            device_id_type=MESH,
        )

    def send(self, src, dst, peer):
        copy = self.make(src, dst, peer, self.block(1))
        copy.start()
        self.sent.append(copy)
        return copy


def sum_and_share(wire, here, make, part, xland, lx, lz, zx, full, residual):
    core, xl, z, zp, zm, xm, cp = here
    base = core * MINE

    def zat(d):
        return lax.rem(z + (d + RING), RING)

    def x_copy(i, first):
        f = (1 - xl) * RING + lax.rem(z + ring_order(i), RING)
        return wire.make(part.at[f, pl.ds(0, HALF)], xland.at[i], xm, first + i)

    first_x = wire.block(RING)

    def x_step(i, carry):
        make((1 - xl) * RING + lax.rem(z + ring_order(i), RING), 0)
        x_copy(i, first_x).start()
        return carry

    lax.fori_loop(0, RING, x_step, 0)

    def z_step(i, carry):
        zz = lax.rem(z + ring_order(i), RING)
        make(2 * zz, 1)
        make(2 * zz + 1, 1)
        return carry

    z_step(0, 0)
    rx = [[None] * 4, [None] * 4]
    rz = [[None] * 4, [None] * 4]
    zrows = [(HALF, QUART), (HALF + QUART, QUART)]
    xrows = [(0, QUART), (QUART, QUART)]
    far = zat(4)
    for way, peer in ((0, zp), (1, zm)):
        lo, n = zrows[way]
        rz[way][0] = wire.send(
            part.at[pl.ds(2 * far, 2), pl.ds(lo, n)],
            lz.at[way, 0, :, pl.ds(lo - HALF, n)],
            peer,
        )
    lax.fori_loop(1, RING, z_step, 0)

    def own_step(i, carry):
        make(xl * RING + lax.rem(z + ring_order(i), RING), 0)
        return carry

    lax.fori_loop(0, RING, own_step, 0)

    def wait_x(i):
        x_copy(i, first_x).wait_recv()

    for k in range(4):
        for way, peer in ((0, zp), (1, zm)):
            zz = zat(4 - k if way == 0 else k - 4)
            f = xl * RING + zz
            if k == 0:
                if way == 0:
                    wait_x(0)
                    part[f, 0:HALF] = (
                        part[f, 0:HALF].astype(F32) + xland[0].astype(F32)
                    ).astype(BF)
                lo, n = xrows[way]
            else:
                i = 2 * k - 1 + way
                wait_x(i)
                rx[way][k - 1].wait_recv()
                for at, (slo, sn) in enumerate(xrows):
                    value = part[f, slo : slo + sn].astype(F32) + xland[i, slo : slo + sn].astype(F32)
                    if k > 1 or at == way:
                        value = value + lx[way, k - 1, slo : slo + sn].astype(F32)
                    part[f, slo : slo + sn] = value.astype(BF)
                lo, n = 0, HALF
            rx[way][k] = wire.send(
                part.at[f, pl.ds(lo, n)], lx.at[way, k, pl.ds(lo, n)], peer
            )
        if k > 0:
            for way, peer in ((0, zp), (1, zm)):
                zz = zat(4 - k if way == 0 else k - 4)
                rz[way][k - 1].wait_recv()
                lo, n = zrows[way] if k == 1 else (HALF, HALF)
                for e in range(2):
                    value = part[2 * zz + e, lo : lo + n].astype(F32)
                    value = value + lz[way, k - 1, e, lo - HALF : lo - HALF + n].astype(F32)
                    part[2 * zz + e, lo : lo + n] = value.astype(BF)
                rz[way][k] = wire.send(
                    part.at[pl.ds(2 * zz, 2), pl.ds(HALF, HALF)], lz.at[way, k], peer
                )

    rz[0][3].wait_recv()
    rz[1][3].wait_recv()

    def z_sum(e):
        return (
            part[2 * z + e, HALF:OWN].astype(F32)
            + lz[0, 3, e].astype(F32)
            + lz[1, 3, e].astype(F32)
        )

    part[2 * z + (1 - xl), HALF:OWN] = z_sum(1 - xl).astype(BF)
    cross = wire.send(part.at[2 * z + (1 - xl), pl.ds(HALF, HALF)], zx, xm)

    wait_x(7)
    rx[0][3].wait_recv()
    rx[1][3].wait_recv()
    f0 = xl * RING + z
    value = part[f0, 0:HALF].astype(F32) + xland[7].astype(F32)
    value = value + lx[0, 3].astype(F32) + lx[1, 3].astype(F32)
    if residual is not None:
        value = value + residual[base + f0, 0:HALF].astype(F32)
    full[base + f0, 0:HALF] = value.astype(BF)

    def xs(zz, lo=0, n=HALF, side=None):
        column = xl if side is None else side
        return full.at[base + column * RING + zz, pl.ds(lo, n)]

    def zs(zz, lo=HALF, n=HALF):
        return full.at[pl.ds(base + 2 * zz, 2), pl.ds(lo, n)]

    def go(ref, peer):
        return wire.send(ref, ref, peer)

    gx = [[go(xs(z), zp)], [go(xs(z), zm)]]
    gxx = [go(xs(z), xm)]
    gc = [go(xs(z), cp)]

    cross.wait_recv()
    value = z_sum(xl) + zx[...].astype(F32)
    mine = 2 * z + xl
    if residual is not None:
        value = value + residual[base + mine, HALF:OWN].astype(F32)
    full[base + mine, HALF:OWN] = value.astype(BF)
    swap = go(full.at[base + mine, pl.ds(HALF, HALF)], xm)
    swap.wait_recv()
    gz = [[go(zs(z), zp)], [go(zs(z), zm)]]
    gc.append(go(zs(z), cp))

    for k in range(1, 5):
        for way, peer in ((0, zp), (1, zm)):
            zz = zat(-k if way == 0 else k)
            gx[way][k - 1].wait_recv()
            if k < 4:
                lo, n = (0, HALF) if k < 3 else xrows[way]
                gx[way].append(go(xs(zz, lo, n), peer))
                gxx.append(go(xs(zz), xm))
                gc.append(go(xs(zz), cp))
        if k == 4:
            gxx.append(go(xs(zat(4)), xm))
            gc.append(go(xs(zat(4)), cp))
        for way, peer in ((0, zp), (1, zm)):
            zz = zat(-k if way == 0 else k)
            gz[way][k - 1].wait_recv()
            if k < 4:
                lo, n = (HALF, HALF) if k < 3 else zrows[way]
                gz[way].append(go(zs(zz, lo, n), peer))
                gc.append(go(zs(zz), cp))
        if k == 4:
            gc.append(go(zs(zat(4)), cp))
        for i in [0] if k == 1 else [2 * k - 3, 2 * k - 2]:
            gxx[i].wait_recv()
            d = (i + 1) // 2 if i % 2 == 0 else -((i + 1) // 2)
            gc.append(go(xs(zat(d), side=1 - xl), cp))
    gxx[7].wait_recv()
    gc.append(go(xs(zat(4), side=1 - xl), cp))
    for copy in gc:
        copy.wait_recv()

    def x_done(i, carry):
        x_copy(i, first_x).wait_send()
        return carry

    lax.fori_loop(0, RING, x_done, 0)


def project(full, gain_ref, weight, acc, squares):
    acc[...] = jnp.zeros_like(acc)
    squares[...] = jnp.zeros_like(squares)
    per = 4

    def step(s, carry):
        total, sq = None, None
        for e in range(per):
            i = s * per + e
            value = full[i].astype(F32)
            term = dot(
                (value * gain_ref[pl.ds(i, 1), :]).astype(BF),
                weight[pl.ds(pl.multiple_of(i * WIDE, WIDE), WIDE), :],
            )
            total = term if total is None else total + term
            sq = value * value if sq is None else sq + value * value
        acc[...] += total
        squares[...] += sq
        return carry

    lax.fori_loop(0, CHUNKS // per, step, 0)
    mean = jnp.sum(squares[...], axis=1, keepdims=True) * (1.0 / (CHUNKS * WIDE))
    return lax.rsqrt(mean + EPSILON)


def kernel(
    info_ref, lens_ref, gain_ref, final_ref, cache_ref, table_ref, wq_ref, wkv_ref, wo_ref, wp_ref,
    out_ref,
    info, tabs, wqkv, wo, wp, member, pack, unpack, onehot, part1, part2, xland1, xland2, lx1, lx2,
    lz1, lz2, zx1, zx2, full1, full2, att, acc, acc2, squares, outgo, back, local_sem, send_sem,
    recv_sem,
):
    g = lax.axis_index("grp")
    t = lax.axis_index("tp")
    core = t % 2
    z = (t // 2) % RING
    xl = t // (2 * RING)

    def place(x, zz, cc):
        return (g, (x * RING + zz) * 2 + cc)

    zp = place(xl, lax.rem(z + 1, RING), core)
    zm = place(xl, lax.rem(z + RING - 1, RING), core)
    xm = place(1 - xl, z, core)
    cp = place(xl, z, 1 - core)
    here = (core, xl, z, zp, zm, xm, cp)
    mates = [(lax.rem(g + k, GROUPS), t) for k in range(1, GROUPS)]

    loads = [
        pltpu.make_async_copy(table_ref, tabs.at[core], local_sem.at[0]),
        pltpu.make_async_copy(wq_ref, wqkv.at[:, pl.ds(0, HEAD)], local_sem.at[1]),
        pltpu.make_async_copy(wkv_ref.at[0], wqkv.at[:, pl.ds(HEAD, HEAD)], local_sem.at[2]),
        pltpu.make_async_copy(wkv_ref.at[1], wqkv.at[:, pl.ds(2 * HEAD, HEAD)], local_sem.at[3]),
        pltpu.make_async_copy(
            wo_ref.at[:, pl.ds(pl.multiple_of(core * MINE * WIDE, WIDE), MINE * WIDE)],
            wo.at[pl.ds(pl.multiple_of(core * HEAD, HEAD), HEAD)],
            local_sem.at[4],
        ),
        pltpu.make_async_copy(wp_ref, wp, local_sem.at[5]),
    ]
    for load in loads:
        load.start()
    info[g] = info_ref[...]

    barrier = pltpu.get_barrier_semaphore()
    peers = [zp, zm, xm, cp] + mates
    for peer in peers:
        pl.semaphore_signal(barrier, inc=1, device_id=peer, device_id_type=MESH)
    pl.semaphore_wait(barrier, len(peers))

    wire = Wire(send_sem, recv_sem)
    told = [wire.send(info.at[g], info.at[g], mate) for mate in mates]
    table_in = wire.send(table_ref, tabs.at[core], cp)
    wo_in = wire.send(
        wo_ref.at[:, pl.ds(pl.multiple_of((1 - core) * MINE * WIDE, WIDE), MINE * WIDE)],
        wo.at[pl.ds(pl.multiple_of(core * HEAD, HEAD), HEAD)],
        cp,
    )
    for copy in told:
        copy.wait_recv()

    slots = lax.broadcasted_iota(jnp.int32, (OWN, LANES), 0) + g * OWN
    codes = jnp.zeros((OWN, 8), F32)
    for e in range(GROUPS):
        hit = (info[e, 8:9, :] == slots).astype(F32).astype(BF)
        member[e] = hit
        codes = codes + dot_lanes(hit, info[e, 0:8, :].astype(F32).astype(BF))
    ids = codes[:, 0:4] * 128.0 + codes[:, 4:8]
    ids = jnp.where(core == 0, ids[:, 0:2], ids[:, 2:4]).astype(jnp.int32)
    ids = ids - (xl * RING + z) * (2 * VOCAB_ROWS)
    names = lax.broadcasted_iota(jnp.int32, (OWN, VOCAB_ROWS), 1)
    for j in range(2):
        for s in range(2):
            onehot[j, s] = (ids[:, j : j + 1] - s * VOCAB_ROWS == names).astype(F32).astype(BF)

    loads[0].wait()
    table_in.wait_recv()

    def embed(f, half):
        rows = pl.ds(half * HALF, HALF)
        j = f // 8
        columns = pl.ds(pl.multiple_of((f % 8) * WIDE, WIDE), WIDE)
        value = dot(onehot[j, 0, rows, :], tabs[0, :, columns])
        value = value + dot(onehot[j, 1, rows, :], tabs[1, :, columns])
        part1[f, rows, :] = value.astype(BF)

    sum_and_share(wire, here, embed, part1, xland1, lx1, lz1, zx1, full1, None)

    for load in loads[1:]:
        load.wait()
    scale = project(full1, gain_ref, wqkv, acc, squares)

    queries = (acc[:, 0:HEAD] * scale).astype(BF).astype(F32)
    keys = (acc[:, HEAD : 2 * HEAD] * scale).astype(BF).astype(F32)
    values = (acc[:, 2 * HEAD :] * scale).astype(BF).astype(F32)
    root = 1.0 / HEAD**0.5
    lens = lens_ref[...]
    scores = []
    for c in range(CACHE):
        s = jnp.sum(queries * cache_ref[0, c].astype(F32), axis=1, keepdims=True) * root
        scores.append(jnp.where(lens > c, s, -1e30))
    scores.append(jnp.sum(queries * keys, axis=1, keepdims=True) * root)
    top = functools.reduce(jnp.maximum, scores)
    raised = [jnp.exp(s - top) for s in scores]
    whole = functools.reduce(jnp.add, raised)
    weights = [(r / whole).astype(BF).astype(F32) for r in raised]
    mixed = weights[CACHE] * values
    for c in range(CACHE):
        mixed = mixed + weights[c] * cache_ref[1, c].astype(F32)
    att[core] = mixed.astype(BF)
    att_in = wire.send(att.at[core], att.at[core], cp)

    upper = (
        lax.broadcasted_iota(jnp.int32, (LANES, LANES), 0)
        <= lax.broadcasted_iota(jnp.int32, (LANES, LANES), 1)
    ).astype(F32).astype(BF)
    places = lax.broadcasted_iota(jnp.int32, (CAP, LANES), 0).astype(F32)
    own_slots = info[g, 8:9, :]
    for e in range(GROUPS):
        row = info[e, 8:9, :] - g * OWN
        inside = ((row >= 0) & (row < OWN)).astype(F32)
        rank = dot(inside.astype(BF), upper)
        pick = jnp.where(rank - 1.0 == places, inside, 0.0).astype(BF)
        pack[e] = dot_lanes(pick, member[e]).astype(BF)
        row = own_slots - e * OWN
        inside = ((row >= 0) & (row < OWN)).astype(F32)
        rank = dot(inside.astype(BF), upper)
        unpack[e] = jnp.where(rank - 1.0 == places, inside, 0.0).astype(BF)

    att_in.wait_recv()
    wo_in.wait_recv()

    def spread(f, half):
        rows = pl.ds(half * HALF, HALF)
        both = jnp.concatenate([att[0, rows, :], att[1, rows, :]], axis=1)
        columns = pl.ds(pl.multiple_of(f * WIDE, WIDE), WIDE)
        part2[f, rows, :] = dot(both, wo[:, columns]).astype(BF)

    sum_and_share(wire, here, spread, part2, xland2, lx2, lz2, zx2, full2, full1)

    scale = project(full2, final_ref, wp, acc2, squares)
    prefix = (acc2[...] * scale).astype(BF)
    homes = []
    for e in range(GROUPS):
        outgo[e] = dot(pack[e], prefix).astype(BF)
    for k, mate in enumerate(mates):
        homes.append(wire.send(outgo.at[mate[0]], back.at[g], mate))
    back[g] = outgo[g]
    for copy in homes:
        copy.wait_recv()
    result = jnp.zeros((LANES, HEAD), F32)
    for e in range(GROUPS):
        result = result + lax.dot_general(
            unpack[e], back[e], (((0,), (0,)), ((), ())), preferred_element_type=F32
        )
    out_ref[...] = result[0:OWN].astype(BF)
    for copy in wire.sent:
        copy.wait_send()


def shards(
    block_tokens, slot_of_row, cache_lengths, embed_table, norm_gain, query_weight, key_value_weight,
    kv_cache, out_weight, final_gain, prefix_weight,
):
    tokens = block_tokens.T
    info = jnp.concatenate([tokens >> 7, tokens & 127, slot_of_row[None, :]], axis=0)
    info = jnp.pad(info, ((0, 16 - 9), (0, LANES - OWN)), constant_values=-1)
    cache = kv_cache.reshape(2, OWN, CACHE, HEAD).transpose(0, 2, 1, 3)
    vmem = pl.BlockSpec(memory_space=pltpu.VMEM)
    hbm = pl.BlockSpec(memory_space=pl.ANY)
    return pl.pallas_call(
        kernel,
        out_shape=jax.ShapeDtypeStruct((OWN, HEAD), BF),
        in_specs=[vmem] * 5 + [hbm] * 5,
        out_specs=vmem,
        scratch_shapes=[
            pltpu.VMEM((GROUPS, 16, LANES), jnp.int32),
            pltpu.VMEM((2, VOCAB_ROWS, 2048), BF),
            pltpu.VMEM((CHUNKS * WIDE, 3 * HEAD), BF),
            pltpu.VMEM((2 * HEAD, MINE * WIDE), BF),
            pltpu.VMEM((CHUNKS * WIDE, HEAD), BF),
            pltpu.VMEM((GROUPS, OWN, LANES), BF),
            pltpu.VMEM((GROUPS, CAP, OWN), BF),
            pltpu.VMEM((GROUPS, CAP, LANES), BF),
            pltpu.VMEM((2, 2, OWN, VOCAB_ROWS), BF),
        ]
        + [pltpu.VMEM((MINE, OWN, WIDE), BF)] * 2
        + [pltpu.VMEM((RING, HALF, WIDE), BF)] * 2
        + [pltpu.VMEM((2, 4, HALF, WIDE), BF)] * 2
        + [pltpu.VMEM((2, 4, 2, HALF, WIDE), BF)] * 2
        + [pltpu.VMEM((HALF, WIDE), BF)] * 2
        + [pltpu.VMEM((CHUNKS, OWN, WIDE), BF)] * 2
        + [
            pltpu.VMEM((2, OWN, HEAD), BF),
            pltpu.VMEM((OWN, 3 * HEAD), F32),
            pltpu.VMEM((OWN, HEAD), F32),
            pltpu.VMEM((OWN, WIDE), F32),
            pltpu.VMEM((GROUPS, CAP, HEAD), BF),
            pltpu.VMEM((GROUPS, CAP, HEAD), BF),
            pltpu.SemaphoreType.DMA((6,)),
            pltpu.SemaphoreType.DMA((SEMS,)),
            pltpu.SemaphoreType.DMA((SEMS,)),
        ],
        compiler_params=pltpu.CompilerParams(
            collective_id=0, has_side_effects=True, vmem_limit_bytes=56 * 1024 * 1024
        ),
    )(
        info,
        cache_lengths[:, None],
        norm_gain.reshape(CHUNKS, WIDE),
        final_gain.reshape(CHUNKS, WIDE),
        cache,
        embed_table,
        query_weight,
        key_value_weight,
        out_weight,
        prefix_weight,
    )


def solution(mesh):
    in_specs = (
        P("grp", None),
        P("grp"),
        P("grp"),
        P("tp", None),
        P(),
        P(None, "tp"),
        P(None, None, "tp"),
        P(None, "grp", None, "tp"),
        P("tp", None),
        P(),
        P(None, "tp"),
    )
    return jax.shard_map(
        shards, mesh=mesh, in_specs=in_specs, out_specs=P("grp", "tp"), check_vma=False
    )
```

```python
import functools

import jax
import jax.numpy as jnp
from jax import lax
from jax.experimental import pallas as pl
from jax.experimental.pallas import tpu as pltpu
from jax.sharding import PartitionSpec as P

MESH = pl.DeviceIdType.MESH
BF = jnp.bfloat16
F32 = jnp.float32
EPSILON = 1e-05
HEAD = 128
CACHE = 4
GROUPS = 8
RING = 8
OWN = 320
HALF = 160
QUART = 80
CAP = 80
LANES = 384
WIDE = 256
CHUNKS = 32
MINE = 16
VOCAB_ROWS = 500
SEMS = 224
QUAD = 4
SPAN = 2048


def dot(a, b):
    return jnp.dot(a, b, preferred_element_type=F32)


def dot_lanes(a, b):
    return lax.dot_general(a, b, (((1,), (1,)), ((), ())), preferred_element_type=F32)


def ring_order(i):
    step = (i + 1) // 2
    return 4 + step * (1 - 2 * (i % 2))


class Wire:
    def __init__(self, send_sem, recv_sem):
        self.send_sem, self.recv_sem = send_sem, recv_sem
        self.used = 0
        self.sent = []

    def block(self, count):
        first = self.used
        self.used += count
        assert self.used <= SEMS
        return first

    def make(self, src, dst, peer, index):
        return pltpu.make_async_remote_copy(
            src_ref=src,
            dst_ref=dst,
            send_sem=self.send_sem.at[index],
            recv_sem=self.recv_sem.at[index],
            device_id=peer,
            device_id_type=MESH,
        )

    def send(self, src, dst, peer):
        copy = self.make(src, dst, peer, self.block(1))
        copy.start()
        self.sent.append(copy)
        return copy


class Ring:
    def __init__(self, wire, here, part, land, streams):
        self.wire, self.here, self.part, self.land, self.streams = wire, here, part, land, streams
        self.got = [[[None] * 4, [None] * 4] for _ in streams]

    def zat(self, d):
        return lax.rem(self.here.z + (d + RING), RING)

    def push(self, s, way, k, f, lo, a, n):
        self.got[s][way][k] = self.wire.send(
            self.part.at[f, pl.ds(lo + a, n)],
            self.land.at[s, way, k, pl.ds(a, n)],
            self.here.zp if way == 0 else self.here.zm,
        )

    def hop0(self, s):
        index, lo, n, far, extra = self.streams[s]
        f = index(self.zat(4))
        if extra is not None:
            rows = slice(lo, lo + n)
            self.part[f, rows] = (self.part[f, rows].astype(F32) + extra(0)).astype(BF)
        for way in range(2):
            a, m = far[way]
            if m:
                self.push(s, way, 0, f, lo, a, m)

    def hop(self, k, s):
        index, lo, n, far, extra = self.streams[s]
        part = self.part
        for way in range(2):
            f = index(self.zat(4 - k if way == 0 else k - 4))
            a, m = far[way] if k == 1 else (0, n)
            if self.got[s][way][k - 1] is not None:
                self.got[s][way][k - 1].wait_recv()
            other = None if extra is None else extra(2 * k - 1 + way)
            cuts = sorted({0, a, a + m, n}) if m else [0, n]
            for lo2, hi2 in zip(cuts[:-1], cuts[1:]):
                landed = m > 0 and lo2 >= a and hi2 <= a + m
                if not landed and other is None:
                    continue
                rows = slice(lo + lo2, lo + hi2)
                value = part[f, rows].astype(F32)
                if other is not None:
                    value = value + other[lo2:hi2]
                if landed:
                    value = value + self.land[s, way, k - 1, lo2:hi2].astype(F32)
                part[f, rows] = value.astype(BF)
            self.push(s, way, k, f, lo, 0, n)

    def total(self, s):
        index, lo, n, far, extra = self.streams[s]
        self.got[s][0][3].wait_recv()
        self.got[s][1][3].wait_recv()
        value = self.part[index(self.here.z), lo : lo + n].astype(F32)
        value = value + self.land[s, 0, 3, 0:n].astype(F32) + self.land[s, 1, 3, 0:n].astype(F32)
        return value if extra is None else value + extra(7)


class Share:
    def __init__(self, wire, here, full, streams):
        self.wire, self.here, self.full, self.streams = wire, here, full, streams
        self.got = [[[], []] for _ in streams]

    def zat(self, d):
        return lax.rem(self.here.z + (d + RING), RING)

    def view(self, s, d, a=0, n=None):
        index, lo, rows, far, tap = self.streams[s]
        return self.full.at[index(self.zat(d)), pl.ds(lo + a, rows if n is None else n)]

    def push(self, s, way, d, a=0, n=None):
        ref = self.view(s, d, a, n)
        peer = self.here.zp if way == 0 else self.here.zm
        self.got[s][way].append(self.wire.send(ref, ref, peer))

    def begin(self, s):
        self.push(s, 0, 0)
        self.push(s, 1, 0)
        if self.streams[s][4] is not None:
            self.streams[s][4](s, 0)

    def hop(self, k, s):
        index, lo, n, far, tap = self.streams[s]
        for way in range(2):
            d = -k if way == 0 else k
            if k == 4:
                if far[way][1]:
                    self.got[s][way][3].wait_recv()
                continue
            self.got[s][way][k - 1].wait_recv()
            if k < 3:
                self.push(s, way, d)
            elif far[way][1]:
                self.push(s, way, d, *far[way])
            if tap is not None:
                tap(s, d)
        if k == 4 and tap is not None:
            tap(s, 4)


SPLIT = ((0, QUART), (QUART, QUART))
UP = ((0, QUART), (0, 0))
DOWN = ((0, 0), (0, QUART))


def sum_and_share(wire, here, make, part, xland, land, zx, full, tag=""):
    core, xl, z = here.core, here.xl, here.z
    base = core * MINE

    def x_copy(i, first):
        f = (1 - xl) * RING + lax.rem(z + ring_order(i), RING)
        return wire.make(part.at[f, pl.ds(0, HALF)], xland.at[i], here.xm, first + i)

    first_x = wire.block(RING)

    def x_step(i, carry):
        make((1 - xl) * RING + lax.rem(z + ring_order(i), RING), 0)
        x_copy(i, first_x).start()
        return carry

    lax.fori_loop(0, RING, x_step, 0)

    def z_step(i, carry):
        zz = lax.rem(z + ring_order(i), RING)
        make(2 * zz, 1)
        make(2 * zz + 1, 1)
        return carry

    def own_step(i, carry):
        make(xl * RING + lax.rem(z + ring_order(i), RING), 0)
        return carry

    def crossed(i):
        x_copy(i, first_x).wait_recv()
        return xland[i].astype(F32)

    streams = [
        (lambda zz: xl * RING + zz, 0, HALF, SPLIT, crossed),
        (lambda zz: 2 * zz + (1 - xl), HALF, HALF, SPLIT, None),
        (lambda zz: 2 * zz + xl, HALF, HALF, SPLIT, None),
    ]
    ring = Ring(wire, here, part, land, streams)
    z_step(0, 0)
    ring.hop0(1)
    ring.hop0(2)
    lax.fori_loop(1, RING, z_step, 0)
    lax.fori_loop(0, RING, own_step, 0)
    ring.hop0(0)
    for k in (1, 2, 3):
        for s in (1, 0, 2):
            ring.hop(k, s)
    away = 2 * z + (1 - xl)
    part[away, HALF:OWN] = ring.total(1).astype(BF)
    cross = wire.send(part.at[away, pl.ds(HALF, HALF)], zx, here.xm)
    full[base + xl * RING + z, 0:HALF] = ring.total(0).astype(BF)

    gxx, gc = {}, []

    def late(s, d):
        ref = share.view(s, d)
        gxx[d] = wire.send(ref, ref, here.xm)
        gc.append(wire.send(ref, ref, here.cp))

    def near(s, d):
        ref = share.view(s, d)
        gc.append(wire.send(ref, ref, here.cp))

    def beside(d):
        gxx[d].wait_recv()
        ref = full.at[base + (1 - xl) * RING + share.zat(d), pl.ds(0, HALF)]
        gc.append(wire.send(ref, ref, here.cp))

    share = Share(
        wire,
        here,
        full,
        [
            (lambda zz: base + xl * RING + zz, 0, HALF, SPLIT, late),
            (lambda zz: base + 2 * zz + xl, HALF, HALF, SPLIT, near),
            (lambda zz: base + 2 * zz + (1 - xl), HALF, HALF, SPLIT, near),
        ],
    )
    share.begin(0)
    value = ring.total(2)
    cross.wait_recv()
    full[base + 2 * z + xl, HALF:OWN] = (value + zx[...].astype(F32)).astype(BF)
    ref = share.view(1, 0)
    swap = wire.send(ref, ref, here.xm)
    share.begin(1)
    swap.wait_recv()
    share.begin(2)
    for k in (1, 2, 3, 4):
        for s in range(3):
            share.hop(k, s)
        for d in [0] if k == 1 else [1 - k, k - 1]:
            beside(d)
    beside(4)
    for copy in gc:
        copy.wait_recv()

    def x_done(i, carry):
        x_copy(i, first_x).wait_send()
        return carry

    lax.fori_loop(0, RING, x_done, 0)


def gain_row(gain_ref, i):
    return jnp.concatenate([gain_ref[pl.ds(2 * i, 1), :], gain_ref[pl.ds(2 * i + 1, 1), :]], axis=1)


def project(full, gain_ref, weight, acc, squares):
    acc[...] = jnp.zeros_like(acc)
    squares[...] = jnp.zeros_like(squares)
    per = 4

    def step(s, carry):
        total, sq = None, None
        for e in range(per):
            i = s * per + e
            value = full[i].astype(F32)
            term = dot(
                (value * gain_row(gain_ref, i)).astype(BF),
                weight[pl.ds(pl.multiple_of(i * WIDE, WIDE), WIDE), :],
            )
            total = term if total is None else total + term
            sq = value * value if sq is None else sq + value * value
        acc[...] += total
        squares[...] += sq
        return carry

    lax.fori_loop(0, CHUNKS // per, step, 0)
    mean = jnp.sum(squares[...], axis=1, keepdims=True) * (1.0 / (CHUNKS * WIDE))
    return lax.rsqrt(mean + EPSILON)


class Here:
    pass


def kernel(
    tokens_ref, slots_ref, lens_ref, gain_ref, final_ref, cache_ref, table_ref, wq_ref, wkv_ref, wo_ref,
    wp_ref, out_ref,
    info, tabs, wqkv, woq, wpq, member, pack, unpack, onehot, natural, cache, part1, part2, xland, land1,
    land2, zx, full1, full2, att, acc, acc4, squares, partial, outgo, back, local_sem, send_sem, recv_sem,
):
    g = lax.axis_index("grp")
    t = lax.axis_index("tp")
    here = Here()
    core = here.core = t % 2
    z = here.z = (t // 2) % RING
    xl = here.xl = t // (2 * RING)
    quarter = core * 2 + xl

    def place(x, zz, cc):
        return (x * RING + zz) * 2 + cc

    here.zp = (g, place(xl, lax.rem(z + 1, RING), core))
    here.zm = (g, place(xl, lax.rem(z + RING - 1, RING), core))
    here.xm = (g, place(1 - xl, z, core))
    here.cp = (g, place(xl, z, 1 - core))
    dg = (g, place(1 - xl, z, 1 - core))
    og = lax.rem(g + GROUPS // 2, GROUPS)
    xm_other = (og, here.xm[1])
    dg_other = (og, dg[1])
    cp_quarter = (1 - core) * 2 + xl
    xm_quarter = core * 2 + (1 - xl)
    dg_quarter = (1 - core) * 2 + (1 - xl)
    mates = [(lax.rem(g + k, GROUPS), t) for k in range(1, GROUPS)]

    def wide(i, n):
        return pl.ds(pl.multiple_of(i * n, n), n)

    table_load = pltpu.make_async_copy(table_ref, tabs.at[core], local_sem.at[0])
    loads = [
        pltpu.make_async_copy(cache_ref, natural, local_sem.at[6]),
        pltpu.make_async_copy(wq_ref, wqkv.at[:, pl.ds(0, HEAD)], local_sem.at[1]),
        pltpu.make_async_copy(wkv_ref.at[0], wqkv.at[:, pl.ds(HEAD, HEAD)], local_sem.at[2]),
        pltpu.make_async_copy(wkv_ref.at[1], wqkv.at[:, pl.ds(2 * HEAD, HEAD)], local_sem.at[3]),
        pltpu.make_async_copy(
            wo_ref.at[:, wide(quarter, SPAN)], woq.at[wide(quarter, HEAD)], local_sem.at[4]
        ),
        pltpu.make_async_copy(
            wp_ref.at[wide(quarter, SPAN)], wpq.at[:, wide(quarter, HEAD)], local_sem.at[5]
        ),
    ]
    table_load.start()
    info[g] = jnp.full((16, LANES), -1, jnp.int32)
    info[g, 0:4, 0:OWN] = tokens_ref[...]
    info[g, 8:9, 0:OWN] = slots_ref[...].reshape(1, OWN)

    barrier = pltpu.get_barrier_semaphore()
    peers = [here.zp, here.zm, here.xm, here.cp, dg, xm_other, dg_other] + mates
    for peer in peers:
        pl.semaphore_signal(barrier, inc=1, device_id=peer, device_id_type=MESH)
    pl.semaphore_wait(barrier, len(peers))

    wire = Wire(send_sem, recv_sem)
    told = [wire.send(info.at[g], info.at[g], mate) for mate in mates]
    table_in = wire.send(table_ref, tabs.at[core], here.cp)
    for load in loads:
        load.start()

    half = SPAN // 2

    def give_wo(who, q, lo, n):
        cols = pl.ds(pl.multiple_of(q * SPAN + lo, half), n)
        return wire.send(wo_ref.at[:, cols], woq.at[wide(quarter, HEAD), pl.ds(lo, n)], who)

    def give_wp(who, q, lo, n):
        rows = pl.ds(pl.multiple_of(q * SPAN + lo, half), n)
        return wire.send(wp_ref.at[rows], wpq.at[pl.ds(lo, n), wide(quarter, HEAD)], who)

    wo_in = [
        give_wo(here.cp, cp_quarter, 0, SPAN),
        give_wo(here.xm, xm_quarter, 0, half),
        give_wo(xm_other, xm_quarter, half, half),
        give_wo(dg, dg_quarter, 0, half),
        give_wo(dg_other, dg_quarter, half, half),
    ]
    for copy in told:
        copy.wait_recv()

    slots = lax.broadcasted_iota(jnp.int32, (OWN, LANES), 0) + g * OWN
    codes = jnp.zeros((OWN, 8), F32)
    for e in range(GROUPS):
        hit = (info[e, 8:9, :] == slots).astype(F32).astype(BF)
        member[e] = hit
        heard = info[e, 0:4, :]
        heard = jnp.concatenate([heard >> 7, heard & 127], axis=0)
        codes = codes + dot_lanes(hit, heard.astype(F32).astype(BF))
    ids = codes[:, 0:4] * 128.0 + codes[:, 4:8]
    ids = jnp.where(core == 0, ids[:, 0:2], ids[:, 2:4]).astype(jnp.int32)
    ids = ids - (xl * RING + z) * (2 * VOCAB_ROWS)
    names = lax.broadcasted_iota(jnp.int32, (OWN, VOCAB_ROWS), 1)
    for j in range(2):
        for s in range(2):
            onehot[j, s] = (ids[:, j : j + 1] - s * VOCAB_ROWS == names).astype(F32).astype(BF)

    table_load.wait()
    table_in.wait_recv()

    def embed(f, side):
        rows = pl.ds(side * HALF, HALF)
        j = f // 8
        columns = wide(f % 8, WIDE)
        value = dot(onehot[j, 0, rows, :], tabs[0, :, columns])
        value = value + dot(onehot[j, 1, rows, :], tabs[1, :, columns])
        part1[f, rows, :] = value.astype(BF)

    sum_and_share(wire, here, embed, part1, xland, land1, zx, full1)

    for load in loads:
        load.wait()
    for k in range(2):
        for b in range(4):
            rows = slice(b * 80, b * 80 + 80)
            block = natural[k, rows].astype(F32)
            for c in range(CACHE):
                cache[k, c, rows] = block[:, c, :].astype(BF)
    scale = project(full1, gain_ref, wqkv, acc, squares)

    queries = (acc[:, 0:HEAD] * scale).astype(BF).astype(F32)
    keys = (acc[:, HEAD : 2 * HEAD] * scale).astype(BF).astype(F32)
    values = (acc[:, 2 * HEAD :] * scale).astype(BF).astype(F32)
    root = 1.0 / HEAD**0.5
    diagonal = lax.broadcasted_iota(jnp.int32, (OWN, OWN), 0) == lax.broadcasted_iota(
        jnp.int32, (OWN, OWN), 1
    )
    lens = jnp.sum(
        jnp.where(diagonal, lens_ref[...].reshape(1, OWN).astype(F32), 0.0), axis=1, keepdims=True
    )
    scores = []
    for c in range(CACHE):
        s = jnp.sum(queries * cache[0, c].astype(F32), axis=1, keepdims=True) * root
        scores.append(jnp.where(lens > c + 0.5, s, -1e30))
    scores.append(jnp.sum(queries * keys, axis=1, keepdims=True) * root)
    top = functools.reduce(jnp.maximum, scores)
    raised = [jnp.exp(s - top) for s in scores]
    whole = functools.reduce(jnp.add, raised)
    weights = [(r / whole).astype(BF).astype(F32) for r in raised]
    mixed = weights[CACHE] * values
    for c in range(CACHE):
        mixed = mixed + weights[c] * cache[1, c].astype(F32)
    att[quarter] = mixed.astype(BF)
    att_in = [wire.send(att.at[quarter], att.at[quarter], who) for who in (here.xm, dg, here.cp)]

    upper = (
        lax.broadcasted_iota(jnp.int32, (LANES, LANES), 0)
        <= lax.broadcasted_iota(jnp.int32, (LANES, LANES), 1)
    ).astype(F32).astype(BF)
    places = lax.broadcasted_iota(jnp.int32, (CAP, LANES), 0).astype(F32)
    own_slots = info[g, 8:9, :]
    for e in range(GROUPS):
        row = info[e, 8:9, :] - g * OWN
        inside = ((row >= 0) & (row < OWN)).astype(F32)
        rank = dot(inside.astype(BF), upper)
        pick = jnp.where(rank - 1.0 == places, inside, 0.0).astype(BF)
        pack[e] = dot_lanes(pick, member[e]).astype(BF)
        row = own_slots - e * OWN
        inside = ((row >= 0) & (row < OWN)).astype(F32)
        rank = dot(inside.astype(BF), upper)
        unpack[e] = jnp.where(rank - 1.0 == places, inside, 0.0).astype(BF)

    for copy in att_in + wo_in:
        copy.wait_recv()
    wp_in = [
        give_wp(here.cp, cp_quarter, 0, SPAN),
        give_wp(here.xm, xm_quarter, 0, half),
        give_wp(xm_other, xm_quarter, half, half),
        give_wp(dg, dg_quarter, 0, half),
        give_wp(dg_other, dg_quarter, half, half),
    ]

    def spread(i, carry):
        zz = lax.rem(z + ring_order(i), RING)
        both = jnp.concatenate([att[q] for q in range(QUAD)], axis=1)
        part2[zz] = dot(both, woq[:, wide(zz, WIDE)]).astype(BF)
        return carry

    strips = [(lambda zz: zz, QUART * s, QUART, (UP, DOWN)[s % 2], None) for s in range(QUAD)]
    ring = Ring(wire, here, part2, land2, strips)
    spread(0, 0)
    for s in range(QUAD):
        ring.hop0(s)
    lax.fori_loop(1, RING, spread, 0)
    for k in (1, 2, 3):
        for s in range(QUAD):
            ring.hop(k, s)
    share = Share(wire, here, full2, strips)
    for s in range(QUAD):
        rows = slice(QUART * s, QUART * s + QUART)
        value = ring.total(s) + full1[quarter * RING + z, rows].astype(F32)
        full2[z, rows] = value.astype(BF)
        share.begin(s)

    def take(zz, first):
        value = full2[zz].astype(F32)
        scaled = (value * gain_row(final_ref, quarter * RING + zz)).astype(BF)
        term = dot(scaled, wpq[wide(zz, WIDE), :])
        if first:
            acc4[...] = term
            squares[...] = value * value
        else:
            acc4[...] += term
            squares[...] += value * value

    for copy in wp_in:
        copy.wait_recv()
    take(z, True)
    for k in (1, 2, 3, 4):
        for s in range(QUAD):
            share.hop(k, s)
        take(share.zat(-k), False)
        if k < 4:
            take(share.zat(k), False)

    square = jnp.sum(squares[...], axis=1, keepdims=True)
    high = square.astype(BF).astype(F32)
    lanes = lax.broadcasted_iota(jnp.int32, (OWN, HEAD), 1)
    tail = jnp.where(lanes < HEAD // 2, high, square - high).astype(BF)
    for q in range(QUAD):
        partial[q, 0] = acc4[:, q * HEAD : (q + 1) * HEAD].astype(BF)
        partial[q, 1] = tail
    sums = [
        wire.send(partial.at[q], back.at[quarter], who)
        for who, q in ((here.xm, xm_quarter), (dg, dg_quarter), (here.cp, cp_quarter))
    ]
    back[quarter] = partial[quarter]
    for copy in sums:
        copy.wait_recv()
    prefix, square = None, None
    for q in range(QUAD):
        term = back[q, 0].astype(F32)
        sq = back[q, 1, :, 0:1].astype(F32) + back[q, 1, :, HEAD // 2 : HEAD // 2 + 1].astype(F32)
        prefix = term if prefix is None else prefix + term
        square = sq if square is None else square + sq
    prefix = (prefix * lax.rsqrt(square * (1.0 / (CHUNKS * WIDE)) + EPSILON)).astype(BF)
    homes = []
    for k, mate in enumerate(mates):
        outgo[mate[0], 0:CAP] = dot(pack[mate[0]], prefix).astype(BF)
        homes.append(wire.send(outgo.at[mate[0], pl.ds(0, CAP)], outgo.at[g, pl.ds(CAP, CAP)], mate))
    outgo[g, CAP : 2 * CAP] = dot(pack[g], prefix).astype(BF)
    for copy in homes:
        copy.wait_recv()
    result = jnp.zeros((LANES, HEAD), F32)
    for e in range(GROUPS):
        result = result + lax.dot_general(
            unpack[e], outgo[e, CAP : 2 * CAP], (((0,), (0,)), ((), ())), preferred_element_type=F32
        )
    out_ref[...] = result[0:OWN].astype(BF)
    for copy in wire.sent:
        copy.wait_send()


def shards(
    block_tokens, slot_of_row, cache_lengths, embed_table, norm_gain, query_weight, key_value_weight,
    kv_cache, out_weight, final_gain, prefix_weight,
):
    vmem = pl.BlockSpec(memory_space=pltpu.VMEM)
    hbm = pl.BlockSpec(memory_space=pl.ANY)
    return pl.pallas_call(
        kernel,
        out_shape=jax.ShapeDtypeStruct((OWN, HEAD), BF),
        in_specs=[vmem] * 5 + [hbm] * 6,
        out_specs=vmem,
        scratch_shapes=[
            pltpu.VMEM((GROUPS, 16, LANES), jnp.int32),
            pltpu.VMEM((2, VOCAB_ROWS, 2048), BF),
            pltpu.VMEM((CHUNKS * WIDE, 3 * HEAD), BF),
            pltpu.VMEM((QUAD * HEAD, SPAN), BF),
            pltpu.VMEM((SPAN, QUAD * HEAD), BF),
            pltpu.VMEM((GROUPS, OWN, LANES), BF),
            pltpu.VMEM((GROUPS, CAP, OWN), BF),
            pltpu.VMEM((GROUPS, CAP, LANES), BF),
            pltpu.VMEM((2, 2, OWN, VOCAB_ROWS), BF),
            pltpu.VMEM((2, OWN, CACHE, HEAD), BF),
            pltpu.VMEM((2, CACHE, OWN, HEAD), BF),
            pltpu.VMEM((MINE, OWN, WIDE), BF),
            pltpu.VMEM((RING, OWN, WIDE), BF),
            pltpu.VMEM((RING, HALF, WIDE), BF),
            pltpu.VMEM((3, 2, 4, HALF, WIDE), BF),
            pltpu.VMEM((QUAD, 2, 4, QUART, WIDE), BF),
            pltpu.VMEM((HALF, WIDE), BF),
            pltpu.VMEM((CHUNKS, OWN, WIDE), BF),
            pltpu.VMEM((RING, OWN, WIDE), BF),
            pltpu.VMEM((QUAD, OWN, HEAD), BF),
            pltpu.VMEM((OWN, 3 * HEAD), F32),
            pltpu.VMEM((OWN, QUAD * HEAD), F32),
            pltpu.VMEM((OWN, WIDE), F32),
            pltpu.VMEM((QUAD, 2, OWN, HEAD), BF),
            pltpu.VMEM((GROUPS, 2 * CAP, HEAD), BF),
            pltpu.VMEM((QUAD, 2, OWN, HEAD), BF),
            pltpu.SemaphoreType.DMA((7,)),
            pltpu.SemaphoreType.DMA((SEMS,)),
            pltpu.SemaphoreType.DMA((SEMS,)),
        ],
        compiler_params=pltpu.CompilerParams(
            collective_id=0, has_side_effects=True, vmem_limit_bytes=56 * 1024 * 1024
        ),
    )(
        block_tokens.T,
        slot_of_row,
        cache_lengths,
        norm_gain.reshape(2 * CHUNKS, HEAD),
        final_gain.reshape(2 * CHUNKS, HEAD),
        kv_cache,
        embed_table,
        query_weight,
        key_value_weight,
        out_weight,
        prefix_weight,
    )


def solution(mesh):
    in_specs = (
        P("grp", None),
        P("grp"),
        P("grp"),
        P("tp", None),
        P(),
        P(None, "tp"),
        P(None, None, "tp"),
        P(None, "grp", None, "tp"),
        P("tp", None),
        P(),
        P(None, "tp"),
    )
    return jax.shard_map(
        shards, mesh=mesh, in_specs=in_specs, out_specs=P("grp", "tp"), check_vma=False
    )
```

```python
import functools

import jax
import jax.numpy as jnp
from jax import lax
from jax.experimental import pallas as pl
from jax.experimental.pallas import tpu as pltpu
from jax.sharding import PartitionSpec as P

MESH = pl.DeviceIdType.MESH
BF = jnp.bfloat16
F32 = jnp.float32
EPSILON = 1e-05
HEAD = 128
CACHE = 4
GROUPS = 8
RING = 8
OWN = 320
HALF = 160
QUART = 80
CAP = 80
LANES = 384
WIDE = 256
CHUNKS = 32
MINE = 16
CORE_SPAN = 1024
VOCAB_ROWS = 500
SEMS = 160
PACK = 80
SLAB = 2 * PACK
NEAR = 7 * SLAB
REST = SLAB
ALL = 8 * SLAB
QKV = 3 * HEAD
PLACES = (0, 2, 4, 6, 7, 5, 3, 1)
FLAG = 16
QUAD = 4
SPAN = 2048


def dot(a, b):
    return jnp.dot(a, b, preferred_element_type=F32)


def dot_lanes(a, b):
    return lax.dot_general(a, b, (((1,), (1,)), ((), ())), preferred_element_type=F32)


def ring_order(i):
    step = (i + 1) // 2
    return 4 + step * (1 - 2 * (i % 2))


class Wire:
    def __init__(self, send_sem, recv_sem):
        self.send_sem, self.recv_sem = send_sem, recv_sem
        self.used = 0
        self.sent = []

    def block(self, count):
        first = self.used
        self.used += count
        assert self.used <= SEMS
        return first

    def make(self, src, dst, peer, index):
        return pltpu.make_async_remote_copy(
            src_ref=src,
            dst_ref=dst,
            send_sem=self.send_sem.at[index],
            recv_sem=self.recv_sem.at[index],
            device_id=peer,
            device_id_type=MESH,
        )

    def send(self, src, dst, peer):
        copy = self.make(src, dst, peer, self.block(1))
        copy.start()
        self.sent.append(copy)
        return copy


class Ring:
    def __init__(self, wire, here, part, land, streams):
        self.wire, self.here, self.part, self.land, self.streams = wire, here, part, land, streams
        self.got = [[[None] * 4, [None] * 4] for _ in streams]

    def zat(self, d):
        return lax.rem(self.here.z + (d + RING), RING)

    def push(self, s, way, k, f, lo, a, n):
        self.got[s][way][k] = self.wire.send(
            self.part.at[f, pl.ds(lo + a, n)],
            self.land.at[s, way, k, pl.ds(a, n)],
            self.here.zp if way == 0 else self.here.zm,
        )

    def hop0(self, s):
        index, lo, n, far, extra = self.streams[s]
        f = index(self.zat(4))
        if extra is not None:
            rows = slice(lo, lo + n)
            self.part[f, rows] = (self.part[f, rows].astype(F32) + extra(0)).astype(BF)
        for way in range(2):
            a, m = far[way]
            if m:
                self.push(s, way, 0, f, lo, a, m)

    def hop(self, k, s):
        index, lo, n, far, extra = self.streams[s]
        part = self.part
        for way in range(2):
            f = index(self.zat(4 - k if way == 0 else k - 4))
            a, m = far[way] if k == 1 else (0, n)
            if self.got[s][way][k - 1] is not None:
                self.got[s][way][k - 1].wait_recv()
            other = None if extra is None else extra(2 * k - 1 + way)
            cuts = sorted({0, a, a + m, n}) if m else [0, n]
            for lo2, hi2 in zip(cuts[:-1], cuts[1:]):
                landed = m > 0 and lo2 >= a and hi2 <= a + m
                if not landed and other is None:
                    continue
                rows = slice(lo + lo2, lo + hi2)
                value = part[f, rows].astype(F32)
                if other is not None:
                    value = value + other[lo2:hi2]
                if landed:
                    value = value + self.land[s, way, k - 1, lo2:hi2].astype(F32)
                part[f, rows] = value.astype(BF)
            self.push(s, way, k, f, lo, 0, n)

    def total(self, s):
        index, lo, n, far, extra = self.streams[s]
        self.got[s][0][3].wait_recv()
        self.got[s][1][3].wait_recv()
        value = self.part[index(self.here.z), lo : lo + n].astype(F32)
        value = value + self.land[s, 0, 3, 0:n].astype(F32) + self.land[s, 1, 3, 0:n].astype(F32)
        return value if extra is None else value + extra(7)


class Share:
    def __init__(self, wire, here, view, streams, seen_from):
        self.wire, self.here, self.view, self.streams, self.seen_from = wire, here, view, streams, seen_from
        self.got = [[[], []] for _ in streams]

    def push(self, s, way, d, a=0, n=None):
        peer, shift = (self.here.zp, -self.seen_from) if way == 0 else (self.here.zm, self.seen_from)
        self.got[s][way].append(
            self.wire.send(self.view(s, d, a, n), self.view(s, d + shift, a, n), peer)
        )

    def begin(self, s):
        self.push(s, 0, 0)
        self.push(s, 1, 0)
        if self.streams[s][1] is not None:
            self.streams[s][1](s, 0)

    def hop(self, k, s):
        far, tap = self.streams[s]
        for way in range(2):
            d = -k if way == 0 else k
            if k == 4:
                if far[way][1]:
                    self.got[s][way][3].wait_recv()
                continue
            self.got[s][way][k - 1].wait_recv()
            if k < 3:
                self.push(s, way, d)
            elif far[way][1]:
                self.push(s, way, d, *far[way])
            if tap is not None:
                tap(s, d)
        if k == 4 and tap is not None:
            tap(s, 4)


SPLIT = ((0, 1), (1, 1))
UP = ((0, QUART), (0, 0))
DOWN = ((0, 0), (0, QUART))


def gain_row(gain_ref, i):
    return jnp.concatenate([gain_ref[pl.ds(2 * i, 1), :], gain_ref[pl.ds(2 * i + 1, 1), :]], axis=1)


class Here:
    pass


def kernel(
    tokens_ref, slots_ref, lens_ref, gain_ref, final_ref, cache_ref, table_ref, wq_ref, wkv_ref, wo_ref,
    wp_ref, out_ref, flag_ref,
    info, tabs, wqkv, folded, product, staged, woq, wpq, member, pack, unpack, upto, packed, near_hot, rest_hot, natural, cache, part2,
    land2, full1, full2, att, acc, acc4, squares, partial, sums_in, outgo, back, local_sem,
    send_sem, recv_sem,
):
    g = lax.axis_index("grp")
    t = lax.axis_index("tp")
    here = Here()
    core = here.core = t % 2
    z = here.z = (t // 2) % RING
    xl = here.xl = t // (2 * RING)
    quarter = core * 2 + xl

    def place(x, zz, cc):
        return (x * RING + zz) * 2 + cc

    here.zp = (g, place(xl, lax.rem(z + 1, RING), core))
    here.zm = (g, place(xl, lax.rem(z + RING - 1, RING), core))
    here.xm = (g, place(1 - xl, z, core))
    here.cp = (g, place(xl, z, 1 - core))
    dg = (g, place(1 - xl, z, 1 - core))
    og = lax.rem(g + GROUPS // 2, GROUPS)
    xm_other = (og, here.xm[1])
    dg_other = (og, dg[1])
    cp_quarter = (1 - core) * 2 + xl
    xm_quarter = core * 2 + (1 - xl)
    dg_quarter = (1 - core) * 2 + (1 - xl)
    mates = [(lax.rem(g + k, GROUPS), t) for k in range(1, GROUPS)]

    def wide(i, n):
        return pl.ds(pl.multiple_of(i * n, n), n)

    def table_half(c):
        return table_ref.at[:, pl.ds(pl.multiple_of(c * CORE_SPAN, CORE_SPAN), CORE_SPAN)]

    table_load = pltpu.make_async_copy(table_half(core), tabs.at[core], local_sem.at[0])
    loads = [
        pltpu.make_async_copy(cache_ref, natural, local_sem.at[6]),
        pltpu.make_async_copy(wq_ref, wqkv.at[:, pl.ds(0, HEAD)], local_sem.at[1]),
        pltpu.make_async_copy(wkv_ref.at[0], wqkv.at[:, pl.ds(HEAD, HEAD)], local_sem.at[2]),
        pltpu.make_async_copy(wkv_ref.at[1], wqkv.at[:, pl.ds(2 * HEAD, HEAD)], local_sem.at[3]),
        pltpu.make_async_copy(wo_ref.at[:, wide(quarter, SPAN)], woq.at[quarter], local_sem.at[4]),
        pltpu.make_async_copy(wp_ref.at[wide(quarter, SPAN)], wpq.at[quarter], local_sem.at[5]),
    ]
    others = [cp_quarter, xm_quarter, dg_quarter]
    stages = [
        pltpu.make_async_copy(wo_ref.at[:, wide(q, SPAN)], staged.at[q], local_sem.at[7 + n])
        for n, q in enumerate(others)
    ]
    table_load.start()
    for stage in stages:
        stage.start()
    info[g] = jnp.full((16, LANES), -1, jnp.int32)
    info[g, 0:4, 0:OWN] = tokens_ref[...]
    info[g, 8:9, 0:OWN] = slots_ref[...].reshape(1, OWN)

    barrier = pltpu.get_barrier_semaphore()
    peers = [here.zp, here.zm, here.xm, here.cp, dg, xm_other, dg_other] + mates
    for peer in peers:
        pl.semaphore_signal(barrier, inc=1, device_id=peer, device_id_type=MESH)
    pl.semaphore_wait(barrier, len(peers))

    wire = Wire(send_sem, recv_sem)
    told = [wire.send(info.at[g], info.at[g], mate) for mate in mates]
    table_in = wire.send(table_half(1 - core), tabs.at[core], here.cp)
    for load in loads:
        load.start()

    for stage in stages:
        stage.wait()
    receivers = list(zip((here.cp, xm_other, dg_other), others))
    wo_in = [wire.send(staged.at[q], woq.at[quarter], who) for who, q in receivers]
    upto[...] = (
        lax.broadcasted_iota(jnp.int32, (512, 512), 0) <= lax.broadcasted_iota(jnp.int32, (512, 512), 1)
    ).astype(F32).astype(BF)
    for copy in told:
        copy.wait_recv()

    slots = lax.broadcasted_iota(jnp.int32, (OWN, LANES), 0) + g * OWN
    down = jnp.zeros((OWN, 8), F32)
    across = jnp.zeros((8, OWN), F32)
    for e in range(GROUPS):
        hit = (info[e, 8:9, :] == slots).astype(F32).astype(BF)
        member[e] = hit
        heard = info[e, 0:4, :]
        heard = jnp.concatenate([heard >> 7, heard & 127], axis=0).astype(F32).astype(BF)
        down = down + dot_lanes(hit, heard)
        across = across + dot_lanes(heard, hit)
    ids = down[:, 0:4] * 128.0 + down[:, 4:8]
    ids_across = across[0:4] * 128.0 + across[4:8]

    local = (ids - ((xl * RING + z) * (2 * VOCAB_ROWS)).astype(F32)).astype(jnp.int32)
    names = lax.broadcasted_iota(jnp.int32, (OWN, 512), 1)
    seen = []
    for e in range(2):
        hits = jnp.zeros((OWN, 512), F32)
        for j in range(4):
            hits = jnp.where(local[:, j : j + 1] - e * VOCAB_ROWS == names, 1.0, hits)
        seen.append(jnp.where(names[0:1] < VOCAB_ROWS, jnp.max(hits, axis=0, keepdims=True), 0.0))
    ranks = dot(jnp.concatenate(seen, axis=0).astype(BF), upto[...])
    ranks = [ranks[0:1], ranks[1:2] + ranks[0:1, 511:512]]
    order = lax.broadcasted_iota(jnp.int32, (PACK, 512), 0).astype(F32) + 1.0
    picks = [jnp.where(ranks[e] == order, seen[e], 0.0).astype(BF)[:, 0:VOCAB_ROWS] for e in range(2)]

    table_load.wait()
    table_in.wait_recv()
    for e in range(4):
        columns = slice(e * WIDE, (e + 1) * WIDE)
        value = dot(picks[0], tabs[0, :, columns]) + dot(picks[1], tabs[1, :, columns])
        packed[core * 4 + e, 0, xl] = value.astype(BF)

    gxx, gc = {}, {}

    def view(s, d, first=0, n=None):
        side = 1 - xl if s == 2 else xl
        at = core * 4 + (0 if s == 0 else 2) + first
        return packed.at[pl.ds(at, 2 if n is None else n), PLACES[d % RING], side]

    def beyond(s, d):
        ref = view(s, d)
        gxx[d] = wire.send(ref, ref, here.xm)
        gc[s, d] = wire.send(ref, ref, here.cp)

    def beside(s, d):
        ref = view(s, d)
        gc[s, d] = wire.send(ref, ref, here.cp)

    def late(d):
        gxx[d].wait_recv()
        ref = packed.at[pl.ds(core * 4, 2), PLACES[d % RING], 1 - xl]
        gc[3, d] = wire.send(ref, ref, here.cp)

    share = Share(wire, here, view, [(SPLIT, beyond), (SPLIT, beside), (SPLIT, beside)], 1)
    ref = view(1, 0)
    swap = wire.send(ref, ref, here.xm)
    share.begin(0)
    share.begin(1)
    for load in loads:
        load.wait()
    for k in range(2):
        for b in range(4):
            rows = slice(b * 80, b * 80 + 80)
            block = natural[k, rows].astype(F32)
            for c in range(CACHE):
                cache[k, c, rows] = block[:, c, :].astype(BF)
    swap.wait_recv()
    share.begin(2)
    for s in range(3):
        share.hop(1, s)
    late(0)

    shares = jnp.floor((ids + 0.5) * (0.5 / VOCAB_ROWS))
    lowest = shares * (2.0 * VOCAB_ROWS)
    earlier = lax.broadcasted_iota(jnp.int32, (OWN, OWN), 0) < lax.broadcasted_iota(
        jnp.int32, (OWN, OWN), 1
    )
    firsts = []
    for j in range(4):
        row = ids_across[j : j + 1]
        again = jnp.where(earlier & (ids[:, j : j + 1] == row), 1.0, 0.0)
        for i in range(j):
            again = jnp.where(ids[:, i : i + 1] == row, 1.0, again)
        firsts.append(jnp.where(jnp.max(again, axis=0, keepdims=True) > 0.0, -1.0, row))
    rank = []
    for j in range(4):
        below = jnp.zeros((OWN, OWN), F32)
        for i in range(4):
            inside = (firsts[i] >= lowest[:, j : j + 1]) & (firsts[i] < ids[:, j : j + 1])
            below = below + jnp.where(inside, 1.0, 0.0)
        rank.append(jnp.sum(below, axis=1, keepdims=True))
    rank = jnp.concatenate(rank, axis=1)
    over = jnp.max(jnp.where(rank >= PACK, 1.0, 0.0))
    column = jnp.where(shares >= RING, 1.0, 0.0)
    apart = shares - column * RING - z.astype(F32)
    apart = jnp.where(apart < 0.0, apart + RING, apart)
    slab = jnp.where(apart < 4.0, 2.0 * apart, jnp.where(apart == 4.0, 7.0, 15.0 - 2.0 * apart))
    spot = (slab * SLAB + column * PACK + rank).astype(jnp.int32)
    for j in range(4):
        near_hot[j] = (
            spot[:, j : j + 1] == lax.broadcasted_iota(jnp.int32, (OWN, NEAR), 1)
        ).astype(F32).astype(BF)
        rest_hot[j] = (
            spot[:, j : j + 1] - NEAR == lax.broadcasted_iota(jnp.int32, (OWN, REST), 1)
        ).astype(F32).astype(BF)

    for s in range(3):
        share.hop(2, s)
    late(-1)
    late(1)

    corner = lax.broadcasted_iota(jnp.int32, (WIDE, WIDE), 0) == lax.broadcasted_iota(
        jnp.int32, (WIDE, WIDE), 1
    )

    def fold(f, carry):
        for j in range(4):
            i = j * 8 + f
            gain = jnp.sum(jnp.where(corner, gain_row(gain_ref, i), 0.0), axis=1, keepdims=True)
            folded[wide(f, WIDE), j * QKV : (j + 1) * QKV] = (
                wqkv[wide(i, WIDE), :].astype(F32) * gain
            ).astype(BF)
        return carry

    lax.fori_loop(0, 8, fold, 0)

    def arrived(*apart):
        for s in range(4):
            for d in apart:
                gc[s, d].wait_recv()

    def multiply(a, b):
        rows = slice(a * SLAB, b * SLAB)
        count = (b - a) * SLAB

        def step(n, carry):
            left = [packed[f, a:b].reshape(count, WIDE) for f in range(8)]
            value = dot(jnp.concatenate(left, axis=1), folded[:, wide(n, WIDE)])
            product[rows, wide(n, WIDE)] = value.astype(BF)
            return carry

        lax.fori_loop(0, 4 * QKV // WIDE, step, 0)
        sq = None
        for f in range(8):
            value = packed[f, a:b].reshape(count, WIDE).astype(F32)
            sq = value * value if sq is None else sq + value * value
        sq = jnp.sum(sq, axis=1, keepdims=True)
        high = sq.astype(BF).astype(F32)
        lanes = lax.broadcasted_iota(jnp.int32, (count, HEAD), 1)
        product[rows, 4 * QKV :] = jnp.where(lanes < HEAD // 2, high, sq - high).astype(BF)

    def pick(hot, rows):
        total = None
        for j in range(4):
            right = [product[rows, j * QKV : (j + 1) * QKV], product[rows, 4 * QKV :]]
            term = dot(hot[j], jnp.concatenate(right, axis=1))
            total = term if total is None else total + term
        return total

    for s in range(3):
        share.hop(3, s)
    late(-2)
    late(2)
    wp_in = [wire.send(wp_ref.at[wide(q, SPAN)], wpq.at[quarter], who) for who, q in receivers]
    arrived(0, -1, 1)
    multiply(0, 3)
    for s in range(3):
        share.hop(4, s)
    late(-3)
    late(3)
    arrived(-2, 2)
    multiply(3, 5)
    late(4)
    arrived(-3, 3)
    multiply(5, 7)
    acc[...] = pick(near_hot, slice(0, NEAR))
    arrived(4)
    multiply(7, 8)
    acc[...] += pick(rest_hot, slice(NEAR, ALL))
    square = acc[:, QKV : QKV + 1] + acc[:, QKV + HEAD // 2 : QKV + HEAD // 2 + 1]
    scale = lax.rsqrt(square * (1.0 / (CHUNKS * WIDE)) + EPSILON)

    queries = (acc[:, 0:HEAD] * scale).astype(BF).astype(F32)
    keys = (acc[:, HEAD : 2 * HEAD] * scale).astype(BF).astype(F32)
    values = (acc[:, 2 * HEAD : QKV] * scale).astype(BF).astype(F32)
    root = 1.0 / HEAD**0.5
    diagonal = lax.broadcasted_iota(jnp.int32, (OWN, OWN), 0) == lax.broadcasted_iota(
        jnp.int32, (OWN, OWN), 1
    )
    lens = jnp.sum(
        jnp.where(diagonal, lens_ref[...].reshape(1, OWN).astype(F32), 0.0), axis=1, keepdims=True
    )
    scores = []
    for c in range(CACHE):
        s = jnp.sum(queries * cache[0, c].astype(F32), axis=1, keepdims=True) * root
        scores.append(jnp.where(lens > c + 0.5, s, -1e30))
    scores.append(jnp.sum(queries * keys, axis=1, keepdims=True) * root)
    top = functools.reduce(jnp.maximum, scores)
    raised = [jnp.exp(s - top) for s in scores]
    whole = functools.reduce(jnp.add, raised)
    weights = [(r / whole).astype(BF).astype(F32) for r in raised]
    mixed = weights[CACHE] * values
    for c in range(CACHE):
        mixed = mixed + weights[c] * cache[1, c].astype(F32)
    att[quarter] = mixed.astype(BF)
    att_in = [wire.send(att.at[quarter], att.at[quarter], who) for who in (here.xm, dg, here.cp)]

    upper = (
        lax.broadcasted_iota(jnp.int32, (LANES, LANES), 0)
        <= lax.broadcasted_iota(jnp.int32, (LANES, LANES), 1)
    ).astype(F32).astype(BF)
    places = lax.broadcasted_iota(jnp.int32, (CAP, LANES), 0).astype(F32)
    own_slots = info[g, 8:9, :]
    for e in range(GROUPS):
        row = info[e, 8:9, :] - g * OWN
        inside = ((row >= 0) & (row < OWN)).astype(F32)
        rank = dot(inside.astype(BF), upper)
        pick = jnp.where(rank - 1.0 == places, inside, 0.0).astype(BF)
        pack[e] = dot_lanes(pick, member[e]).astype(BF)
        row = own_slots - e * OWN
        inside = ((row >= 0) & (row < OWN)).astype(F32)
        rank = dot(inside.astype(BF), upper)
        unpack[e] = jnp.where(rank - 1.0 == places, inside, 0.0).astype(BF)

    def lay(f, carry):
        full1[f] = (
            dot(near_hot[quarter], packed[f, 0:7].reshape(NEAR, WIDE))
            + dot(rest_hot[quarter], packed[f, 7].reshape(REST, WIDE))
        ).astype(BF)
        return carry

    lax.fori_loop(0, 8, lay, 0)
    for copy in att_in + wo_in:
        copy.wait_recv()

    def spread(i, carry):
        zz = lax.rem(z + ring_order(i), RING)
        both = jnp.concatenate([att[q] for q in range(QUAD)], axis=1)
        blocks = [woq[q, :, wide(zz, WIDE)] for q in range(QUAD)]
        part2[zz] = dot(both, jnp.concatenate(blocks, axis=0)).astype(BF)
        return carry

    strips = [(lambda zz: zz, QUART * s, QUART, (UP, DOWN)[s % 2], None) for s in range(QUAD)]
    ring = Ring(wire, here, part2, land2, strips)
    spread(0, 0)
    for s in range(QUAD):
        ring.hop0(s)
    lax.fori_loop(1, RING, spread, 0)
    for k in (1, 2, 3):
        for s in range(QUAD):
            ring.hop(k, s)

    def strip(s, d, first=0, n=QUART):
        return full2.at[ring.zat(d), pl.ds(QUART * s + first, n)]

    share = Share(
        wire, here, lambda s, d, a, n: strip(s, d, 0, QUART), [(far, None) for _, _, _, far, _ in strips], 0
    )
    for s in range(QUAD):
        rows = slice(QUART * s, QUART * s + QUART)
        value = ring.total(s) + full1[z, rows].astype(F32)
        full2[z, rows] = value.astype(BF)
        share.begin(s)

    def take(zz, first):
        value = full2[zz].astype(F32)
        scaled = (value * gain_row(final_ref, quarter * RING + zz)).astype(BF)
        blocks = [wpq[q, wide(zz, WIDE), :] for q in range(QUAD)]
        term = dot(scaled, jnp.concatenate(blocks, axis=1))
        if first:
            acc4[...] = term
            squares[...] = value * value
        else:
            acc4[...] += term
            squares[...] += value * value

    for copy in wp_in:
        copy.wait_recv()
    take(z, True)
    for k in (1, 2, 3, 4):
        for s in range(QUAD):
            share.hop(k, s)
        take(ring.zat(-k), False)
        if k < 4:
            take(ring.zat(k), False)

    for q in range(QUAD):
        partial[q] = acc4[:, q * HEAD : (q + 1) * HEAD].astype(BF)
    mine = [
        wire.send(partial.at[q], back.at[quarter], who)
        for who, q in ((here.xm, xm_quarter), (dg, dg_quarter), (here.cp, cp_quarter))
    ]
    square = lax.dot_general(
        jnp.ones((8, WIDE), F32),
        squares[...],
        (((1,), (1,)), ((), ())),
        preferred_element_type=F32,
        precision=lax.Precision.HIGHEST,
    )
    sums_in[quarter] = square
    mine += [
        wire.send(sums_in.at[quarter], sums_in.at[quarter], who) for who in (here.xm, dg, here.cp)
    ]
    back[quarter] = partial[quarter]
    for copy in mine:
        copy.wait_recv()
    prefix, square = None, None
    for q in range(QUAD):
        term = back[q].astype(F32)
        prefix = term if prefix is None else prefix + term
        square = sums_in[q, 0:1] if square is None else square + sums_in[q, 0:1]
    square = lax.rsqrt(square * (1.0 / (CHUNKS * WIDE)) + EPSILON)
    square = jnp.sum(jnp.where(diagonal, square, 0.0), axis=1, keepdims=True)
    prefix = (prefix * square).astype(BF)
    homes = []
    away = CAP + FLAG
    for e in range(GROUPS):
        outgo[e, CAP:away] = jnp.full((FLAG, HEAD), over, F32).astype(BF)
    for k, mate in enumerate(mates):
        outgo[mate[0], 0:CAP] = dot(pack[mate[0]], prefix).astype(BF)
        homes.append(wire.send(outgo.at[mate[0], pl.ds(0, away)], outgo.at[g, pl.ds(away, away)], mate))
    outgo[g, away : away + CAP] = dot(pack[g], prefix).astype(BF)
    outgo[g, away + CAP : 2 * away] = jnp.full((FLAG, HEAD), over, F32).astype(BF)
    for copy in homes:
        copy.wait_recv()
    result = jnp.zeros((LANES, HEAD), F32)
    flag = jnp.zeros((FLAG, HEAD), F32)
    for e in range(GROUPS):
        flag = jnp.maximum(flag, outgo[e, away + CAP : 2 * away].astype(F32))
        result = result + lax.dot_general(
            unpack[e], outgo[e, away : away + CAP], (((0,), (0,)), ((), ())), preferred_element_type=F32
        )
    out_ref[...] = result[0:OWN].astype(BF)
    flag_ref[...] = flag[0:8].astype(jnp.int32)
    for copy in wire.sent:
        copy.wait_send()


def sum_shares(rows):
    count = lax.axis_size("tp")
    blocks = rows.reshape(rows.shape[0], count, -1).transpose(1, 0, 2)
    blocks = lax.all_to_all(blocks, "tp", split_axis=0, concat_axis=0, tiled=True)
    return jnp.sum(blocks.astype(jnp.float32), axis=0)


def all_shares(rows):
    count = lax.axis_size("tp")
    blocks = jnp.broadcast_to(rows[None], (count,) + rows.shape)
    blocks = lax.all_to_all(blocks, "tp", split_axis=0, concat_axis=0, tiled=True)
    return blocks.transpose(1, 0, 2).reshape(rows.shape[0], -1)


def rms_scale(rows, gain):
    values = rows.astype(jnp.float32)
    spread = jnp.mean(values * values, axis=-1, keepdims=True)
    return (values * lax.rsqrt(spread + EPSILON) * gain).astype(jnp.bfloat16)


def routing(slot_ids, owned, groups, capacity):
    target = slot_ids // owned
    place_in = slot_ids % owned
    member = (target[:, None] == jnp.arange(groups, dtype=jnp.int32)[None, :]).astype(jnp.int32)
    within = jnp.sum((jnp.cumsum(member, axis=0) - 1) * member, axis=1)
    return (target * capacity + within, place_in)


def pack_rows(values, slot_index, total):
    buffer = jnp.zeros((total,) + values.shape[1:], values.dtype)
    return buffer.at[slot_index].set(values)


def lookup_part(token_ids, table):
    vocab_rows = table.shape[0]
    local_ids = token_ids - lax.axis_index("tp") * vocab_rows
    inside = (local_ids >= 0) & (local_ids < vocab_rows)
    picked = jnp.take(table, jnp.clip(local_ids, 0, vocab_rows - 1), axis=0)
    picked = jnp.where(inside[..., None], picked, jnp.zeros_like(picked))
    return picked.reshape(token_ids.shape[0], -1).astype(jnp.float32)


def attend(normed, query_weight, key_value_weight, kv_cache, cache_lengths):
    row_count = normed.shape[0]
    queries = jnp.dot(normed, query_weight, preferred_element_type=jnp.float32).astype(jnp.bfloat16)
    fresh = jnp.einsum(
        "rg,kgd->krd", normed, key_value_weight, preferred_element_type=jnp.float32
    ).astype(jnp.bfloat16)
    heads_here = queries.shape[1] // HEAD
    query_heads = queries.reshape(row_count, heads_here, HEAD)
    key_heads = fresh[0].reshape(row_count, heads_here, HEAD)
    value_heads = fresh[1].reshape(row_count, heads_here, HEAD)
    cached = kv_cache.reshape(2, row_count, CACHE, heads_here, HEAD)
    scale = 1.0 / HEAD**0.5
    past = (
        jnp.einsum("rhd,rchd->rhc", query_heads, cached[0], preferred_element_type=jnp.float32)
        * scale
    )
    valid = jnp.arange(CACHE, dtype=jnp.int32)[None, None, :] < cache_lengths[:, None, None]
    past = jnp.where(valid, past, jnp.float32(-1e30))
    own_score = (
        jnp.sum(query_heads.astype(jnp.float32) * key_heads.astype(jnp.float32), axis=-1)[..., None]
        * scale
    )
    weights = jax.nn.softmax(jnp.concatenate([past, own_score], axis=-1), axis=-1).astype(
        jnp.bfloat16
    )
    mixed = jnp.einsum(
        "rhc,rchd->rhd", weights[..., :-1], cached[1], preferred_element_type=jnp.float32
    )
    mixed = mixed + weights[..., -1:].astype(jnp.float32) * value_heads.astype(jnp.float32)
    return mixed.reshape(row_count, -1).astype(jnp.bfloat16)


def plain(
    block_tokens,
    slot_of_row,
    cache_lengths,
    embed_table,
    norm_gain,
    query_weight,
    key_value_weight,
    kv_cache,
    out_weight,
    final_gain,
    prefix_weight,
):
    groups = lax.axis_size("grp")
    owned = slot_of_row.shape[0]
    capacity = 2 * owned // groups
    total = groups * capacity
    slot_index, place_in = routing(slot_of_row, owned, groups, capacity)
    sent_place = (
        jnp.full((total,), owned, jnp.int32).at[slot_index].set(place_in).reshape(groups, capacity)
    )
    shares = sum_shares(lookup_part(block_tokens, embed_table).astype(jnp.bfloat16)).astype(jnp.bfloat16)
    sent_rows = pack_rows(shares, slot_index, total).reshape(groups, capacity, -1)
    got_rows, got_place = (
        lax.all_to_all(sent_rows, "grp", split_axis=0, concat_axis=0, tiled=True),
        lax.all_to_all(sent_place, "grp", split_axis=0, concat_axis=0, tiled=True),
    )
    got_place = got_place.reshape(total)
    own_part = (
        jnp.zeros((owned, shares.shape[1]), jnp.bfloat16)
        .at[got_place]
        .set(got_rows.reshape(total, -1), mode="drop")
    )
    whole = all_shares(own_part)
    normed = rms_scale(whole, norm_gain)
    attended = attend(normed, query_weight, key_value_weight, kv_cache, cache_lengths)
    partial_value = jnp.dot(attended, out_weight, preferred_element_type=jnp.float32)
    summed = sum_shares(partial_value.astype(jnp.bfloat16))
    context = (own_part.astype(jnp.float32) + summed).astype(jnp.bfloat16)
    source_rows = jnp.minimum(got_place, owned - 1)
    back_rows = jnp.take(context, source_rows, axis=0).reshape(groups, capacity, -1)
    home_rows = lax.all_to_all(back_rows, "grp", split_axis=0, concat_axis=0, tiled=True).reshape(
        total, -1
    )
    mine = jnp.take(home_rows, slot_index, axis=0)
    full_rows = all_shares(mine)
    return jnp.dot(
        rms_scale(full_rows, final_gain), prefix_weight, preferred_element_type=jnp.float32
    ).astype(jnp.bfloat16)


def shards(
    block_tokens, slot_of_row, cache_lengths, embed_table, norm_gain, query_weight, key_value_weight,
    kv_cache, out_weight, final_gain, prefix_weight,
):
    vmem = pl.BlockSpec(memory_space=pltpu.VMEM)
    hbm = pl.BlockSpec(memory_space=pl.ANY)
    out, flag = pl.pallas_call(
        kernel,
        out_shape=[jax.ShapeDtypeStruct((OWN, HEAD), BF), jax.ShapeDtypeStruct((8, HEAD), jnp.int32)],
        in_specs=[vmem] * 5 + [hbm] * 6,
        out_specs=[vmem, vmem],
        scratch_shapes=[
            pltpu.VMEM((GROUPS, 16, LANES), jnp.int32),
            pltpu.VMEM((2, VOCAB_ROWS, CORE_SPAN), BF),
            pltpu.VMEM((CHUNKS * WIDE, 3 * HEAD), BF),
            pltpu.VMEM((SPAN, 4 * QKV), BF),
            pltpu.VMEM((ALL, 4 * QKV + HEAD), BF),
            pltpu.VMEM((QUAD, HEAD, SPAN), BF),
            pltpu.VMEM((QUAD, HEAD, SPAN), BF),
            pltpu.VMEM((QUAD, SPAN, HEAD), BF),
            pltpu.VMEM((GROUPS, OWN, LANES), BF),
            pltpu.VMEM((GROUPS, CAP, OWN), BF),
            pltpu.VMEM((GROUPS, CAP, LANES), BF),
            pltpu.VMEM((512, 512), BF),
            pltpu.VMEM((8, RING, 2, PACK, WIDE), BF),
            pltpu.VMEM((4, OWN, NEAR), BF),
            pltpu.VMEM((4, OWN, REST), BF),
            pltpu.VMEM((2, OWN, CACHE, HEAD), BF),
            pltpu.VMEM((2, CACHE, OWN, HEAD), BF),
            pltpu.VMEM((RING, OWN, WIDE), BF),
            pltpu.VMEM((QUAD, 2, 4, QUART, WIDE), BF),
            pltpu.VMEM((RING, OWN, WIDE), BF),
            pltpu.VMEM((RING, OWN, WIDE), BF),
            pltpu.VMEM((QUAD, OWN, HEAD), BF),
            pltpu.VMEM((OWN, QUAD * HEAD), F32),
            pltpu.VMEM((OWN, QUAD * HEAD), F32),
            pltpu.VMEM((OWN, WIDE), F32),
            pltpu.VMEM((QUAD, OWN, HEAD), BF),
            pltpu.VMEM((QUAD, 8, OWN), F32),
            pltpu.VMEM((GROUPS, 2 * (CAP + FLAG), HEAD), BF),
            pltpu.VMEM((QUAD, OWN, HEAD), BF),
            pltpu.SemaphoreType.DMA((10,)),
            pltpu.SemaphoreType.DMA((SEMS,)),
            pltpu.SemaphoreType.DMA((SEMS,)),
        ],
        compiler_params=pltpu.CompilerParams(
            collective_id=0, has_side_effects=True, vmem_limit_bytes=60 * 1024 * 1024
        ),
    )(
        block_tokens.T,
        slot_of_row,
        cache_lengths,
        norm_gain.reshape(2 * CHUNKS, HEAD),
        final_gain.reshape(2 * CHUNKS, HEAD),
        kv_cache,
        embed_table,
        query_weight,
        key_value_weight,
        out_weight,
        prefix_weight,
    )
    return lax.cond(
        flag[0, 0] > 0,
        lambda: plain(
            block_tokens, slot_of_row, cache_lengths, embed_table, norm_gain, query_weight,
            key_value_weight, kv_cache, out_weight, final_gain, prefix_weight,
        ),
        lambda: out,
    )


def solution(mesh):
    in_specs = (
        P("grp", None),
        P("grp"),
        P("grp"),
        P("tp", None),
        P(),
        P(None, "tp"),
        P(None, None, "tp"),
        P(None, "grp", None, "tp"),
        P("tp", None),
        P(),
        P(None, "tp"),
    )
    return jax.shard_map(
        shards, mesh=mesh, in_specs=in_specs, out_specs=P("grp", "tp"), check_vma=False
    )
```

```python
import functools

import jax
import jax.numpy as jnp
from jax import lax
from jax.experimental import pallas as pl
from jax.experimental.pallas import tpu as pltpu
from jax.sharding import PartitionSpec as P

MESH = pl.DeviceIdType.MESH
BF = jnp.bfloat16
F32 = jnp.float32
EPSILON = 1e-05
HEAD = 128
CACHE = 4
GROUPS = 8
RING = 8
OWN = 320
HALF = 160
QUART = 80
CAP = 80
LANES = 384
WIDE = 256
CHUNKS = 32
MINE = 16
CORE_SPAN = 1024
VOCAB_ROWS = 500
SEMS = 160
PACK = 80
SLAB = 2 * PACK
NEAR = 7 * SLAB
REST = SLAB
ALL = 8 * SLAB
QKV = 3 * HEAD
PLACES = (0, 2, 4, 6, 7, 5, 3, 1)
FLAG = 16
QUAD = 4
SPAN = 2048


def dot(a, b):
    return jnp.dot(a, b, preferred_element_type=F32)


def dot_lanes(a, b):
    return lax.dot_general(a, b, (((1,), (1,)), ((), ())), preferred_element_type=F32)


def ring_order(i):
    step = (i + 1) // 2
    return 4 + step * (1 - 2 * (i % 2))


class Wire:
    def __init__(self, send_sem, recv_sem):
        self.send_sem, self.recv_sem = send_sem, recv_sem
        self.used = 0
        self.sent = []

    def block(self, count):
        first = self.used
        self.used += count
        assert self.used <= SEMS
        return first

    def make(self, src, dst, peer, index):
        return pltpu.make_async_remote_copy(
            src_ref=src,
            dst_ref=dst,
            send_sem=self.send_sem.at[index],
            recv_sem=self.recv_sem.at[index],
            device_id=peer,
            device_id_type=MESH,
        )

    def send(self, src, dst, peer):
        copy = self.make(src, dst, peer, self.block(1))
        copy.start()
        self.sent.append(copy)
        return copy


class Ring:
    def __init__(self, wire, here, part, land, streams):
        self.wire, self.here, self.part, self.land, self.streams = wire, here, part, land, streams
        self.got = [[[None] * 4, [None] * 4] for _ in streams]

    def zat(self, d):
        return lax.rem(self.here.z + (d + RING), RING)

    def push(self, s, way, k, f, lo, a, n):
        self.got[s][way][k] = self.wire.send(
            self.part.at[f, pl.ds(lo + a, n)],
            self.land.at[s, way, k, pl.ds(a, n)],
            self.here.zp if way == 0 else self.here.zm,
        )

    def hop0(self, s):
        index, lo, n, far, extra = self.streams[s]
        f = index(self.zat(4))
        if extra is not None:
            rows = slice(lo, lo + n)
            self.part[f, rows] = (self.part[f, rows].astype(F32) + extra(0)).astype(BF)
        for way in range(2):
            a, m = far[way]
            if m:
                self.push(s, way, 0, f, lo, a, m)

    def hop(self, k, s):
        index, lo, n, far, extra = self.streams[s]
        part = self.part
        for way in range(2):
            f = index(self.zat(4 - k if way == 0 else k - 4))
            a, m = far[way] if k == 1 else (0, n)
            if self.got[s][way][k - 1] is not None:
                self.got[s][way][k - 1].wait_recv()
            other = None if extra is None else extra(2 * k - 1 + way)
            cuts = sorted({0, a, a + m, n}) if m else [0, n]
            for lo2, hi2 in zip(cuts[:-1], cuts[1:]):
                landed = m > 0 and lo2 >= a and hi2 <= a + m
                if not landed and other is None:
                    continue
                rows = slice(lo + lo2, lo + hi2)
                value = part[f, rows].astype(F32)
                if other is not None:
                    value = value + other[lo2:hi2]
                if landed:
                    value = value + self.land[s, way, k - 1, lo2:hi2].astype(F32)
                part[f, rows] = value.astype(BF)
            self.push(s, way, k, f, lo, 0, n)

    def total(self, s):
        index, lo, n, far, extra = self.streams[s]
        self.got[s][0][3].wait_recv()
        self.got[s][1][3].wait_recv()
        value = self.part[index(self.here.z), lo : lo + n].astype(F32)
        value = value + self.land[s, 0, 3, 0:n].astype(F32) + self.land[s, 1, 3, 0:n].astype(F32)
        return value if extra is None else value + extra(7)


class Share:
    def __init__(self, wire, here, view, streams, seen_from):
        self.wire, self.here, self.view, self.streams, self.seen_from = wire, here, view, streams, seen_from
        self.got = [[[], []] for _ in streams]

    def push(self, s, way, d, a=0, n=None):
        peer, shift = (self.here.zp, -self.seen_from) if way == 0 else (self.here.zm, self.seen_from)
        self.got[s][way].append(
            self.wire.send(self.view(s, d, a, n), self.view(s, d + shift, a, n), peer)
        )

    def begin(self, s):
        self.push(s, 0, 0)
        self.push(s, 1, 0)
        if self.streams[s][1] is not None:
            self.streams[s][1](s, 0)

    def hop(self, k, s):
        far, tap = self.streams[s]
        for way in range(2):
            d = -k if way == 0 else k
            if k == 4:
                if far[way][1]:
                    self.got[s][way][3].wait_recv()
                continue
            self.got[s][way][k - 1].wait_recv()
            if k < 3:
                self.push(s, way, d)
            elif far[way][1]:
                self.push(s, way, d, *far[way])
            if tap is not None:
                tap(s, d)
        if k == 4 and tap is not None:
            tap(s, 4)


SPLIT = ((0, 1), (1, 1))
UP = ((0, QUART), (0, 0))
DOWN = ((0, 0), (0, QUART))


def gain_row(gain_ref, i):
    return jnp.concatenate([gain_ref[pl.ds(2 * i, 1), :], gain_ref[pl.ds(2 * i + 1, 1), :]], axis=1)


class Here:
    pass


def kernel(
    tokens_ref, slots_ref, lens_ref, gain_ref, final_ref, cache_ref, table_ref, wq_ref, wkv_ref, wo_ref,
    wp_ref, out_ref, flag_ref,
    info, tabs, wqkv, folded, product, staged, woq, wpq, member, pack, unpack, upto, packed, near_hot, rest_hot, natural, cache, part2,
    land2, full1, full2, att, acc, acc4, squares, partial, sums_in, outgo, back, local_sem,
    send_sem, recv_sem,
):
    g = lax.axis_index("grp")
    t = lax.axis_index("tp")
    here = Here()
    core = here.core = t % 2
    z = here.z = (t // 2) % RING
    xl = here.xl = t // (2 * RING)
    quarter = core * 2 + xl

    def place(x, zz, cc):
        return (x * RING + zz) * 2 + cc

    here.zp = (g, place(xl, lax.rem(z + 1, RING), core))
    here.zm = (g, place(xl, lax.rem(z + RING - 1, RING), core))
    here.xm = (g, place(1 - xl, z, core))
    here.cp = (g, place(xl, z, 1 - core))
    dg = (g, place(1 - xl, z, 1 - core))
    og = lax.rem(g + GROUPS // 2, GROUPS)
    xm_other = (og, here.xm[1])
    dg_other = (og, dg[1])
    cp_quarter = (1 - core) * 2 + xl
    xm_quarter = core * 2 + (1 - xl)
    dg_quarter = (1 - core) * 2 + (1 - xl)
    mates = [(lax.rem(g + k, GROUPS), t) for k in range(1, GROUPS)]

    def wide(i, n):
        return pl.ds(pl.multiple_of(i * n, n), n)

    def table_half(c):
        return table_ref.at[:, pl.ds(pl.multiple_of(c * CORE_SPAN, CORE_SPAN), CORE_SPAN)]

    table_load = pltpu.make_async_copy(table_half(core), tabs.at[core], local_sem.at[0])
    loads = [
        pltpu.make_async_copy(cache_ref, natural, local_sem.at[6]),
        pltpu.make_async_copy(wq_ref, wqkv.at[:, pl.ds(0, HEAD)], local_sem.at[1]),
        pltpu.make_async_copy(wkv_ref.at[0], wqkv.at[:, pl.ds(HEAD, HEAD)], local_sem.at[2]),
        pltpu.make_async_copy(wkv_ref.at[1], wqkv.at[:, pl.ds(2 * HEAD, HEAD)], local_sem.at[3]),
        pltpu.make_async_copy(wo_ref.at[:, wide(quarter, SPAN)], woq.at[quarter], local_sem.at[4]),
        pltpu.make_async_copy(wp_ref.at[wide(quarter, SPAN)], wpq.at[quarter], local_sem.at[5]),
    ]
    others = [cp_quarter, xm_quarter, dg_quarter]
    stages = [
        pltpu.make_async_copy(wo_ref.at[:, wide(q, SPAN)], staged.at[q], local_sem.at[7 + n])
        for n, q in enumerate(others)
    ]
    table_load.start()
    for copy in stages + loads:
        copy.start()
    info[g] = jnp.full((16, LANES), -1, jnp.int32)
    info[g, 0:4, 0:OWN] = tokens_ref[...]
    info[g, 8:9, 0:OWN] = slots_ref[...].reshape(1, OWN)

    barrier = pltpu.get_barrier_semaphore()
    peers = [here.zp, here.zm, here.xm, here.cp, dg, xm_other, dg_other] + mates
    for peer in peers:
        pl.semaphore_signal(barrier, inc=1, device_id=peer, device_id_type=MESH)
    pl.semaphore_wait(barrier, len(peers))

    wire = Wire(send_sem, recv_sem)
    told = [wire.send(info.at[g], info.at[g], mate) for mate in mates]
    table_in = wire.send(table_half(1 - core), tabs.at[core], here.cp)

    for stage in stages:
        stage.wait()
    receivers = list(zip((here.cp, xm_other, dg_other), others))
    wo_in = [wire.send(staged.at[q], woq.at[quarter], who) for who, q in receivers]
    upto[...] = (
        lax.broadcasted_iota(jnp.int32, (512, 512), 0) <= lax.broadcasted_iota(jnp.int32, (512, 512), 1)
    ).astype(F32).astype(BF)
    for load in loads:
        load.wait()
    for k in range(2):
        for b in range(4):
            rows = slice(b * 80, b * 80 + 80)
            block = natural[k, rows].astype(F32)
            for c in range(CACHE):
                cache[k, c, rows] = block[:, c, :].astype(BF)

    corner = lax.broadcasted_iota(jnp.int32, (WIDE, WIDE), 0) == lax.broadcasted_iota(
        jnp.int32, (WIDE, WIDE), 1
    )

    def fold(f, carry):
        for j in range(4):
            i = j * 8 + f
            gain = jnp.sum(jnp.where(corner, gain_row(gain_ref, i), 0.0), axis=1, keepdims=True)
            folded[wide(f, WIDE), j * QKV : (j + 1) * QKV] = (
                wqkv[wide(i, WIDE), :].astype(F32) * gain
            ).astype(BF)
        return carry

    lax.fori_loop(0, 8, fold, 0)
    for copy in told:
        copy.wait_recv()

    slots = lax.broadcasted_iota(jnp.int32, (OWN, LANES), 0) + g * OWN
    down = jnp.zeros((OWN, 8), F32)
    across = jnp.zeros((8, OWN), F32)
    for e in range(GROUPS):
        hit = (info[e, 8:9, :] == slots).astype(F32).astype(BF)
        member[e] = hit
        heard = info[e, 0:4, :]
        heard = jnp.concatenate([heard >> 7, heard & 127], axis=0).astype(F32).astype(BF)
        down = down + dot_lanes(hit, heard)
        across = across + dot_lanes(heard, hit)
    ids = down[:, 0:4] * 128.0 + down[:, 4:8]
    ids_across = across[0:4] * 128.0 + across[4:8]

    local = (ids - ((xl * RING + z) * (2 * VOCAB_ROWS)).astype(F32)).astype(jnp.int32)
    names = lax.broadcasted_iota(jnp.int32, (OWN, 512), 1)
    seen = []
    for e in range(2):
        hits = jnp.zeros((OWN, 512), F32)
        for j in range(4):
            hits = jnp.where(local[:, j : j + 1] - e * VOCAB_ROWS == names, 1.0, hits)
        seen.append(jnp.where(names[0:1] < VOCAB_ROWS, jnp.max(hits, axis=0, keepdims=True), 0.0))
    ranks = dot(jnp.concatenate(seen, axis=0).astype(BF), upto[...])
    ranks = [ranks[0:1], ranks[1:2] + ranks[0:1, 511:512]]
    order = lax.broadcasted_iota(jnp.int32, (PACK, 512), 0).astype(F32) + 1.0
    picks = [jnp.where(ranks[e] == order, seen[e], 0.0).astype(BF)[:, 0:VOCAB_ROWS] for e in range(2)]

    table_load.wait()
    table_in.wait_recv()
    for e in range(4):
        columns = slice(e * WIDE, (e + 1) * WIDE)
        value = dot(picks[0], tabs[0, :, columns]) + dot(picks[1], tabs[1, :, columns])
        packed[core * 4 + e, 0, xl] = value.astype(BF)

    gxx, gc = {}, {}

    def view(s, d, first=0, n=None):
        side = 1 - xl if s == 2 else xl
        at = core * 4 + (0 if s == 0 else 2) + first
        return packed.at[pl.ds(at, 2 if n is None else n), PLACES[d % RING], side]

    def beyond(s, d):
        ref = view(s, d)
        gxx[d] = wire.send(ref, ref, here.xm)
        gc[s, d] = wire.send(ref, ref, here.cp)

    def beside(s, d):
        ref = view(s, d)
        gc[s, d] = wire.send(ref, ref, here.cp)

    def late(d):
        gxx[d].wait_recv()
        ref = packed.at[pl.ds(core * 4, 2), PLACES[d % RING], 1 - xl]
        gc[3, d] = wire.send(ref, ref, here.cp)

    share = Share(wire, here, view, [(SPLIT, beyond), (SPLIT, beside), (SPLIT, beside)], 1)
    ref = view(1, 0)
    swap = wire.send(ref, ref, here.xm)
    share.begin(0)
    share.begin(1)
    swap.wait_recv()
    share.begin(2)
    for s in range(3):
        share.hop(1, s)
    late(0)

    shares = jnp.floor((ids + 0.5) * (0.5 / VOCAB_ROWS))
    lowest = shares * (2.0 * VOCAB_ROWS)
    earlier = lax.broadcasted_iota(jnp.int32, (OWN, OWN), 0) < lax.broadcasted_iota(
        jnp.int32, (OWN, OWN), 1
    )
    firsts = []
    for j in range(4):
        row = ids_across[j : j + 1]
        again = jnp.where(earlier & (ids[:, j : j + 1] == row), 1.0, 0.0)
        for i in range(j):
            again = jnp.where(ids[:, i : i + 1] == row, 1.0, again)
        firsts.append(jnp.where(jnp.max(again, axis=0, keepdims=True) > 0.0, -1.0, row))
    rank = []
    for j in range(4):
        below = jnp.zeros((OWN, OWN), F32)
        for i in range(4):
            inside = (firsts[i] >= lowest[:, j : j + 1]) & (firsts[i] < ids[:, j : j + 1])
            below = below + jnp.where(inside, 1.0, 0.0)
        rank.append(jnp.sum(below, axis=1, keepdims=True))
    rank = jnp.concatenate(rank, axis=1)
    over = jnp.max(jnp.where(rank >= PACK, 1.0, 0.0))
    column = jnp.where(shares >= RING, 1.0, 0.0)
    apart = shares - column * RING - z.astype(F32)
    apart = jnp.where(apart < 0.0, apart + RING, apart)
    slab = jnp.where(apart < 4.0, 2.0 * apart, jnp.where(apart == 4.0, 7.0, 15.0 - 2.0 * apart))
    spot = (slab * SLAB + column * PACK + rank).astype(jnp.int32)
    for j in range(4):
        near_hot[j] = (
            spot[:, j : j + 1] == lax.broadcasted_iota(jnp.int32, (OWN, NEAR), 1)
        ).astype(F32).astype(BF)
        rest_hot[j] = (
            spot[:, j : j + 1] - NEAR == lax.broadcasted_iota(jnp.int32, (OWN, REST), 1)
        ).astype(F32).astype(BF)

    for s in range(3):
        share.hop(2, s)
    late(-1)
    late(1)

    def arrived(*apart):
        for s in range(4):
            for d in apart:
                gc[s, d].wait_recv()

    def multiply(a, b):
        rows = slice(a * SLAB, b * SLAB)
        count = (b - a) * SLAB

        def step(n, carry):
            left = [packed[f, a:b].reshape(count, WIDE) for f in range(8)]
            value = dot(jnp.concatenate(left, axis=1), folded[:, wide(n, WIDE)])
            product[rows, wide(n, WIDE)] = value.astype(BF)
            return carry

        lax.fori_loop(0, 4 * QKV // WIDE, step, 0)
        sq = None
        for f in range(8):
            value = packed[f, a:b].reshape(count, WIDE).astype(F32)
            sq = value * value if sq is None else sq + value * value
        sq = jnp.sum(sq, axis=1, keepdims=True)
        high = sq.astype(BF).astype(F32)
        lanes = lax.broadcasted_iota(jnp.int32, (count, HEAD), 1)
        product[rows, 4 * QKV :] = jnp.where(lanes < HEAD // 2, high, sq - high).astype(BF)

    def pick(hot, rows):
        total = None
        for j in range(4):
            right = [product[rows, j * QKV : (j + 1) * QKV], product[rows, 4 * QKV :]]
            term = dot(hot[j], jnp.concatenate(right, axis=1))
            total = term if total is None else total + term
        return total

    for s in range(3):
        share.hop(3, s)
    late(-2)
    late(2)
    wp_in = [wire.send(wp_ref.at[wide(q, SPAN)], wpq.at[quarter], who) for who, q in receivers]
    arrived(0, -1, 1)
    multiply(0, 3)
    for s in range(3):
        share.hop(4, s)
    late(-3)
    late(3)
    arrived(-2, 2)
    multiply(3, 5)
    late(4)
    arrived(-3, 3)
    multiply(5, 7)
    acc[...] = pick(near_hot, slice(0, NEAR))
    arrived(4)
    multiply(7, 8)
    acc[...] += pick(rest_hot, slice(NEAR, ALL))
    square = acc[:, QKV : QKV + 1] + acc[:, QKV + HEAD // 2 : QKV + HEAD // 2 + 1]
    scale = lax.rsqrt(square * (1.0 / (CHUNKS * WIDE)) + EPSILON)

    queries = (acc[:, 0:HEAD] * scale).astype(BF).astype(F32)
    keys = (acc[:, HEAD : 2 * HEAD] * scale).astype(BF).astype(F32)
    values = (acc[:, 2 * HEAD : QKV] * scale).astype(BF).astype(F32)
    root = 1.0 / HEAD**0.5
    diagonal = lax.broadcasted_iota(jnp.int32, (OWN, OWN), 0) == lax.broadcasted_iota(
        jnp.int32, (OWN, OWN), 1
    )
    lens = jnp.sum(
        jnp.where(diagonal, lens_ref[...].reshape(1, OWN).astype(F32), 0.0), axis=1, keepdims=True
    )
    scores = []
    for c in range(CACHE):
        s = jnp.sum(queries * cache[0, c].astype(F32), axis=1, keepdims=True) * root
        scores.append(jnp.where(lens > c + 0.5, s, -1e30))
    scores.append(jnp.sum(queries * keys, axis=1, keepdims=True) * root)
    top = functools.reduce(jnp.maximum, scores)
    raised = [jnp.exp(s - top) for s in scores]
    whole = functools.reduce(jnp.add, raised)
    weights = [(r / whole).astype(BF).astype(F32) for r in raised]
    mixed = weights[CACHE] * values
    for c in range(CACHE):
        mixed = mixed + weights[c] * cache[1, c].astype(F32)
    att[quarter] = mixed.astype(BF)
    att_in = [wire.send(att.at[quarter], att.at[quarter], who) for who in (here.xm, dg, here.cp)]

    def lay(f, carry):
        full1[f] = (
            dot(near_hot[quarter], packed[f, 0:7].reshape(NEAR, WIDE))
            + dot(rest_hot[quarter], packed[f, 7].reshape(REST, WIDE))
        ).astype(BF)
        return carry

    lax.fori_loop(0, 8, lay, 0)
    for copy in att_in + wo_in:
        copy.wait_recv()

    def spread(i, carry):
        zz = lax.rem(z + ring_order(i), RING)
        both = jnp.concatenate([att[q] for q in range(QUAD)], axis=1)
        blocks = [woq[q, :, wide(zz, WIDE)] for q in range(QUAD)]
        part2[zz] = dot(both, jnp.concatenate(blocks, axis=0)).astype(BF)
        return carry

    strips = [(lambda zz: zz, QUART * s, QUART, (UP, DOWN)[s % 2], None) for s in range(QUAD)]
    ring = Ring(wire, here, part2, land2, strips)
    spread(0, 0)
    for s in range(QUAD):
        ring.hop0(s)
    lax.fori_loop(1, RING, spread, 0)
    for k in (1, 2, 3):
        for s in range(QUAD):
            ring.hop(k, s)

    def strip(s, d, first=0, n=QUART):
        return full2.at[ring.zat(d), pl.ds(QUART * s + first, n)]

    share = Share(
        wire, here, lambda s, d, a, n: strip(s, d, 0, QUART), [(far, None) for _, _, _, far, _ in strips], 0
    )
    for s in range(QUAD):
        rows = slice(QUART * s, QUART * s + QUART)
        value = ring.total(s) + full1[z, rows].astype(F32)
        full2[z, rows] = value.astype(BF)
        share.begin(s)

    def take(zz, first):
        value = full2[zz].astype(F32)
        scaled = (value * gain_row(final_ref, quarter * RING + zz)).astype(BF)
        blocks = [wpq[q, wide(zz, WIDE), :] for q in range(QUAD)]
        term = dot(scaled, jnp.concatenate(blocks, axis=1))
        if first:
            acc4[...] = term
            squares[...] = value * value
        else:
            acc4[...] += term
            squares[...] += value * value

    upper = (
        lax.broadcasted_iota(jnp.int32, (LANES, LANES), 0)
        <= lax.broadcasted_iota(jnp.int32, (LANES, LANES), 1)
    ).astype(F32).astype(BF)
    places = lax.broadcasted_iota(jnp.int32, (CAP, LANES), 0).astype(F32)
    own_slots = info[g, 8:9, :]
    for e in range(GROUPS):
        row = info[e, 8:9, :] - g * OWN
        inside = ((row >= 0) & (row < OWN)).astype(F32)
        rank = dot(inside.astype(BF), upper)
        pick = jnp.where(rank - 1.0 == places, inside, 0.0).astype(BF)
        pack[e] = dot_lanes(pick, member[e]).astype(BF)
        row = own_slots - e * OWN
        inside = ((row >= 0) & (row < OWN)).astype(F32)
        rank = dot(inside.astype(BF), upper)
        unpack[e] = jnp.where(rank - 1.0 == places, inside, 0.0).astype(BF)

    for copy in wp_in:
        copy.wait_recv()
    take(z, True)
    for k in (1, 2, 3, 4):
        for s in range(QUAD):
            share.hop(k, s)
        take(ring.zat(-k), False)
        if k < 4:
            take(ring.zat(k), False)

    for q in range(QUAD):
        partial[q] = acc4[:, q * HEAD : (q + 1) * HEAD].astype(BF)
    mine = [
        wire.send(partial.at[q], back.at[quarter], who)
        for who, q in ((here.xm, xm_quarter), (dg, dg_quarter), (here.cp, cp_quarter))
    ]
    square = lax.dot_general(
        jnp.ones((8, WIDE), F32),
        squares[...],
        (((1,), (1,)), ((), ())),
        preferred_element_type=F32,
        precision=lax.Precision.HIGHEST,
    )
    sums_in[quarter] = square
    mine += [
        wire.send(sums_in.at[quarter], sums_in.at[quarter], who) for who in (here.xm, dg, here.cp)
    ]
    back[quarter] = partial[quarter]
    for copy in mine:
        copy.wait_recv()
    prefix, square = None, None
    for q in range(QUAD):
        term = back[q].astype(F32)
        prefix = term if prefix is None else prefix + term
        square = sums_in[q, 0:1] if square is None else square + sums_in[q, 0:1]
    square = lax.rsqrt(square * (1.0 / (CHUNKS * WIDE)) + EPSILON)
    square = jnp.sum(jnp.where(diagonal, square, 0.0), axis=1, keepdims=True)
    prefix = (prefix * square).astype(BF)
    homes = []
    away = CAP + FLAG
    for e in range(GROUPS):
        outgo[e, CAP:away] = jnp.full((FLAG, HEAD), over, F32).astype(BF)
    for k, mate in enumerate(mates):
        outgo[mate[0], 0:CAP] = dot(pack[mate[0]], prefix).astype(BF)
        homes.append(wire.send(outgo.at[mate[0], pl.ds(0, away)], outgo.at[g, pl.ds(away, away)], mate))
    outgo[g, away : away + CAP] = dot(pack[g], prefix).astype(BF)
    outgo[g, away + CAP : 2 * away] = jnp.full((FLAG, HEAD), over, F32).astype(BF)
    for copy in homes:
        copy.wait_recv()
    result = jnp.zeros((LANES, HEAD), F32)
    flag = jnp.zeros((FLAG, HEAD), F32)
    for e in range(GROUPS):
        flag = jnp.maximum(flag, outgo[e, away + CAP : 2 * away].astype(F32))
        result = result + lax.dot_general(
            unpack[e], outgo[e, away : away + CAP], (((0,), (0,)), ((), ())), preferred_element_type=F32
        )
    out_ref[...] = result[0:OWN].astype(BF)
    flag_ref[0, 0] = jnp.max(flag).astype(jnp.int32)
    for copy in wire.sent:
        copy.wait_send()


def sum_shares(rows):
    count = lax.axis_size("tp")
    blocks = rows.reshape(rows.shape[0], count, -1).transpose(1, 0, 2)
    blocks = lax.all_to_all(blocks, "tp", split_axis=0, concat_axis=0, tiled=True)
    return jnp.sum(blocks.astype(jnp.float32), axis=0)


def all_shares(rows):
    count = lax.axis_size("tp")
    blocks = jnp.broadcast_to(rows[None], (count,) + rows.shape)
    blocks = lax.all_to_all(blocks, "tp", split_axis=0, concat_axis=0, tiled=True)
    return blocks.transpose(1, 0, 2).reshape(rows.shape[0], -1)


def rms_scale(rows, gain):
    values = rows.astype(jnp.float32)
    spread = jnp.mean(values * values, axis=-1, keepdims=True)
    return (values * lax.rsqrt(spread + EPSILON) * gain).astype(jnp.bfloat16)


def routing(slot_ids, owned, groups, capacity):
    target = slot_ids // owned
    place_in = slot_ids % owned
    member = (target[:, None] == jnp.arange(groups, dtype=jnp.int32)[None, :]).astype(jnp.int32)
    within = jnp.sum((jnp.cumsum(member, axis=0) - 1) * member, axis=1)
    return (target * capacity + within, place_in)


def pack_rows(values, slot_index, total):
    buffer = jnp.zeros((total,) + values.shape[1:], values.dtype)
    return buffer.at[slot_index].set(values)


def lookup_part(token_ids, table):
    vocab_rows = table.shape[0]
    local_ids = token_ids - lax.axis_index("tp") * vocab_rows
    inside = (local_ids >= 0) & (local_ids < vocab_rows)
    picked = jnp.take(table, jnp.clip(local_ids, 0, vocab_rows - 1), axis=0)
    picked = jnp.where(inside[..., None], picked, jnp.zeros_like(picked))
    return picked.reshape(token_ids.shape[0], -1).astype(jnp.float32)


def attend(normed, query_weight, key_value_weight, kv_cache, cache_lengths):
    row_count = normed.shape[0]
    queries = jnp.dot(normed, query_weight, preferred_element_type=jnp.float32).astype(jnp.bfloat16)
    fresh = jnp.einsum(
        "rg,kgd->krd", normed, key_value_weight, preferred_element_type=jnp.float32
    ).astype(jnp.bfloat16)
    heads_here = queries.shape[1] // HEAD
    query_heads = queries.reshape(row_count, heads_here, HEAD)
    key_heads = fresh[0].reshape(row_count, heads_here, HEAD)
    value_heads = fresh[1].reshape(row_count, heads_here, HEAD)
    cached = kv_cache.reshape(2, row_count, CACHE, heads_here, HEAD)
    scale = 1.0 / HEAD**0.5
    past = (
        jnp.einsum("rhd,rchd->rhc", query_heads, cached[0], preferred_element_type=jnp.float32)
        * scale
    )
    valid = jnp.arange(CACHE, dtype=jnp.int32)[None, None, :] < cache_lengths[:, None, None]
    past = jnp.where(valid, past, jnp.float32(-1e30))
    own_score = (
        jnp.sum(query_heads.astype(jnp.float32) * key_heads.astype(jnp.float32), axis=-1)[..., None]
        * scale
    )
    weights = jax.nn.softmax(jnp.concatenate([past, own_score], axis=-1), axis=-1).astype(
        jnp.bfloat16
    )
    mixed = jnp.einsum(
        "rhc,rchd->rhd", weights[..., :-1], cached[1], preferred_element_type=jnp.float32
    )
    mixed = mixed + weights[..., -1:].astype(jnp.float32) * value_heads.astype(jnp.float32)
    return mixed.reshape(row_count, -1).astype(jnp.bfloat16)


def plain(
    block_tokens,
    slot_of_row,
    cache_lengths,
    embed_table,
    norm_gain,
    query_weight,
    key_value_weight,
    kv_cache,
    out_weight,
    final_gain,
    prefix_weight,
):
    groups = lax.axis_size("grp")
    owned = slot_of_row.shape[0]
    capacity = 2 * owned // groups
    total = groups * capacity
    slot_index, place_in = routing(slot_of_row, owned, groups, capacity)
    sent_place = (
        jnp.full((total,), owned, jnp.int32).at[slot_index].set(place_in).reshape(groups, capacity)
    )
    shares = sum_shares(lookup_part(block_tokens, embed_table).astype(jnp.bfloat16)).astype(jnp.bfloat16)
    sent_rows = pack_rows(shares, slot_index, total).reshape(groups, capacity, -1)
    got_rows, got_place = (
        lax.all_to_all(sent_rows, "grp", split_axis=0, concat_axis=0, tiled=True),
        lax.all_to_all(sent_place, "grp", split_axis=0, concat_axis=0, tiled=True),
    )
    got_place = got_place.reshape(total)
    own_part = (
        jnp.zeros((owned, shares.shape[1]), jnp.bfloat16)
        .at[got_place]
        .set(got_rows.reshape(total, -1), mode="drop")
    )
    whole = all_shares(own_part)
    normed = rms_scale(whole, norm_gain)
    attended = attend(normed, query_weight, key_value_weight, kv_cache, cache_lengths)
    partial_value = jnp.dot(attended, out_weight, preferred_element_type=jnp.float32)
    summed = sum_shares(partial_value.astype(jnp.bfloat16))
    context = (own_part.astype(jnp.float32) + summed).astype(jnp.bfloat16)
    source_rows = jnp.minimum(got_place, owned - 1)
    back_rows = jnp.take(context, source_rows, axis=0).reshape(groups, capacity, -1)
    home_rows = lax.all_to_all(back_rows, "grp", split_axis=0, concat_axis=0, tiled=True).reshape(
        total, -1
    )
    mine = jnp.take(home_rows, slot_index, axis=0)
    full_rows = all_shares(mine)
    return jnp.dot(
        rms_scale(full_rows, final_gain), prefix_weight, preferred_element_type=jnp.float32
    ).astype(jnp.bfloat16)


def shards(
    block_tokens, slot_of_row, cache_lengths, embed_table, norm_gain, query_weight, key_value_weight,
    kv_cache, out_weight, final_gain, prefix_weight,
):
    vmem = pl.BlockSpec(memory_space=pltpu.VMEM)
    hbm = pl.BlockSpec(memory_space=pl.ANY)
    out, flag = pl.pallas_call(
        kernel,
        out_shape=[jax.ShapeDtypeStruct((OWN, HEAD), BF), jax.ShapeDtypeStruct((1, 1), jnp.int32)],
        in_specs=[vmem] * 5 + [hbm] * 6,
        out_specs=[vmem, pl.BlockSpec(memory_space=pltpu.SMEM)],
        scratch_shapes=[
            pltpu.VMEM((GROUPS, 16, LANES), jnp.int32),
            pltpu.VMEM((2, VOCAB_ROWS, CORE_SPAN), BF),
            pltpu.VMEM((CHUNKS * WIDE, 3 * HEAD), BF),
            pltpu.VMEM((SPAN, 4 * QKV), BF),
            pltpu.VMEM((ALL, 4 * QKV + HEAD), BF),
            pltpu.VMEM((QUAD, HEAD, SPAN), BF),
            pltpu.VMEM((QUAD, HEAD, SPAN), BF),
            pltpu.VMEM((QUAD, SPAN, HEAD), BF),
            pltpu.VMEM((GROUPS, OWN, LANES), BF),
            pltpu.VMEM((GROUPS, CAP, OWN), BF),
            pltpu.VMEM((GROUPS, CAP, LANES), BF),
            pltpu.VMEM((512, 512), BF),
            pltpu.VMEM((8, RING, 2, PACK, WIDE), BF),
            pltpu.VMEM((4, OWN, NEAR), BF),
            pltpu.VMEM((4, OWN, REST), BF),
            pltpu.VMEM((2, OWN, CACHE, HEAD), BF),
            pltpu.VMEM((2, CACHE, OWN, HEAD), BF),
            pltpu.VMEM((RING, OWN, WIDE), BF),
            pltpu.VMEM((QUAD, 2, 4, QUART, WIDE), BF),
            pltpu.VMEM((RING, OWN, WIDE), BF),
            pltpu.VMEM((RING, OWN, WIDE), BF),
            pltpu.VMEM((QUAD, OWN, HEAD), BF),
            pltpu.VMEM((OWN, QUAD * HEAD), F32),
            pltpu.VMEM((OWN, QUAD * HEAD), F32),
            pltpu.VMEM((OWN, WIDE), F32),
            pltpu.VMEM((QUAD, OWN, HEAD), BF),
            pltpu.VMEM((QUAD, 8, OWN), F32),
            pltpu.VMEM((GROUPS, 2 * (CAP + FLAG), HEAD), BF),
            pltpu.VMEM((QUAD, OWN, HEAD), BF),
            pltpu.SemaphoreType.DMA((10,)),
            pltpu.SemaphoreType.DMA((SEMS,)),
            pltpu.SemaphoreType.DMA((SEMS,)),
        ],
        compiler_params=pltpu.CompilerParams(
            collective_id=0, has_side_effects=True, vmem_limit_bytes=60 * 1024 * 1024
        ),
    )(
        block_tokens.T,
        slot_of_row,
        cache_lengths,
        norm_gain.reshape(2 * CHUNKS, HEAD),
        final_gain.reshape(2 * CHUNKS, HEAD),
        kv_cache,
        embed_table,
        query_weight,
        key_value_weight,
        out_weight,
        prefix_weight,
    )
    return lax.cond(
        flag[0, 0] > 0,
        lambda: plain(
            block_tokens, slot_of_row, cache_lengths, embed_table, norm_gain, query_weight,
            key_value_weight, kv_cache, out_weight, final_gain, prefix_weight,
        ),
        lambda: out,
    )


def solution(mesh):
    in_specs = (
        P("grp", None),
        P("grp"),
        P("grp"),
        P("tp", None),
        P(),
        P(None, "tp"),
        P(None, None, "tp"),
        P(None, "grp", None, "tp"),
        P("tp", None),
        P(),
        P(None, "tp"),
    )
    return jax.shard_map(
        shards, mesh=mesh, in_specs=in_specs, out_specs=P("grp", "tp"), check_vma=False
    )
```

```python
import functools

import jax
import jax.numpy as jnp
from jax import lax
from jax.experimental import pallas as pl
from jax.experimental.pallas import tpu as pltpu
from jax.sharding import PartitionSpec as P

MESH = pl.DeviceIdType.MESH
BF = jnp.bfloat16
F32 = jnp.float32
EPSILON = 1e-05
HEAD = 128
CACHE = 4
GROUPS = 8
RING = 8
OWN = 320
HALF = 160
QUART = 80
CAP = 80
LANES = 384
WIDE = 256
CHUNKS = 32
MINE = 16
CORE_SPAN = 1024
VOCAB_ROWS = 500
SEMS = 160
PACK = 80
SLAB = 2 * PACK
NEAR = 7 * SLAB
REST = SLAB
ALL = 8 * SLAB
QKV = 3 * HEAD
PLACES = (0, 2, 4, 6, 7, 5, 3, 1)
FLAG = 16
QUAD = 4
SPAN = 2048


def dot(a, b):
    return jnp.dot(a, b, preferred_element_type=F32)


def dot_lanes(a, b):
    return lax.dot_general(a, b, (((1,), (1,)), ((), ())), preferred_element_type=F32)


def ring_order(i):
    step = (i + 1) // 2
    return 4 + step * (1 - 2 * (i % 2))


class Wire:
    def __init__(self, send_sem, recv_sem):
        self.send_sem, self.recv_sem = send_sem, recv_sem
        self.used = 0
        self.sent = []

    def block(self, count):
        first = self.used
        self.used += count
        assert self.used <= SEMS
        return first

    def make(self, src, dst, peer, index):
        return pltpu.make_async_remote_copy(
            src_ref=src,
            dst_ref=dst,
            send_sem=self.send_sem.at[index],
            recv_sem=self.recv_sem.at[index],
            device_id=peer,
            device_id_type=MESH,
        )

    def send(self, src, dst, peer):
        copy = self.make(src, dst, peer, self.block(1))
        copy.start()
        self.sent.append(copy)
        return copy


class Ring:
    def __init__(self, wire, here, part, land, streams):
        self.wire, self.here, self.part, self.land, self.streams = wire, here, part, land, streams
        self.got = [[[None] * 4, [None] * 4] for _ in streams]

    def zat(self, d):
        return lax.rem(self.here.z + (d + RING), RING)

    def push(self, s, way, k, f, lo, a, n):
        self.got[s][way][k] = self.wire.send(
            self.part.at[f, pl.ds(lo + a, n)],
            self.land.at[s, way, k, pl.ds(a, n)],
            self.here.zp if way == 0 else self.here.zm,
        )

    def hop0(self, s):
        index, lo, n, far, extra = self.streams[s]
        f = index(self.zat(4))
        if extra is not None:
            rows = slice(lo, lo + n)
            self.part[f, rows] = (self.part[f, rows].astype(F32) + extra(0)).astype(BF)
        for way in range(2):
            a, m = far[way]
            if m:
                self.push(s, way, 0, f, lo, a, m)

    def hop(self, k, s):
        index, lo, n, far, extra = self.streams[s]
        part = self.part
        for way in range(2):
            f = index(self.zat(4 - k if way == 0 else k - 4))
            a, m = far[way] if k == 1 else (0, n)
            if self.got[s][way][k - 1] is not None:
                self.got[s][way][k - 1].wait_recv()
            other = None if extra is None else extra(2 * k - 1 + way)
            cuts = sorted({0, a, a + m, n}) if m else [0, n]
            for lo2, hi2 in zip(cuts[:-1], cuts[1:]):
                landed = m > 0 and lo2 >= a and hi2 <= a + m
                if not landed and other is None:
                    continue
                rows = slice(lo + lo2, lo + hi2)
                value = part[f, rows].astype(F32)
                if other is not None:
                    value = value + other[lo2:hi2]
                if landed:
                    value = value + self.land[s, way, k - 1, lo2:hi2].astype(F32)
                part[f, rows] = value.astype(BF)
            self.push(s, way, k, f, lo, 0, n)

    def total(self, s):
        index, lo, n, far, extra = self.streams[s]
        self.got[s][0][3].wait_recv()
        self.got[s][1][3].wait_recv()
        value = self.part[index(self.here.z), lo : lo + n].astype(F32)
        value = value + self.land[s, 0, 3, 0:n].astype(F32) + self.land[s, 1, 3, 0:n].astype(F32)
        return value if extra is None else value + extra(7)


class Share:
    def __init__(self, wire, here, view, streams, seen_from):
        self.wire, self.here, self.view, self.streams, self.seen_from = wire, here, view, streams, seen_from
        self.got = [[[], []] for _ in streams]

    def push(self, s, way, d, a=0, n=None):
        peer, shift = (self.here.zp, -self.seen_from) if way == 0 else (self.here.zm, self.seen_from)
        self.got[s][way].append(
            self.wire.send(self.view(s, d, a, n), self.view(s, d + shift, a, n), peer)
        )

    def begin(self, s):
        self.push(s, 0, 0)
        self.push(s, 1, 0)
        if self.streams[s][1] is not None:
            self.streams[s][1](s, 0)

    def hop(self, k, s):
        far, tap = self.streams[s]
        for way in range(2):
            d = -k if way == 0 else k
            if k == 4:
                if far[way][1]:
                    self.got[s][way][3].wait_recv()
                continue
            self.got[s][way][k - 1].wait_recv()
            if k < 3:
                self.push(s, way, d)
            elif far[way][1]:
                self.push(s, way, d, *far[way])
            if tap is not None:
                tap(s, d)
        if k == 4 and tap is not None:
            tap(s, 4)


SPLIT = ((0, 1), (1, 1))
UP = ((0, QUART), (0, 0))
DOWN = ((0, 0), (0, QUART))


def gain_row(gain_ref, i):
    return jnp.concatenate([gain_ref[pl.ds(2 * i, 1), :], gain_ref[pl.ds(2 * i + 1, 1), :]], axis=1)


class Here:
    pass


def kernel(
    tokens_ref, slots_ref, lens_ref, gain_ref, final_ref, cache_ref, table_ref, wq_ref, wkv_ref, wo_ref,
    wp_ref, out_ref, flag_ref,
    info, tabs, wqkv, folded, product, staged, woq, wpq, member, pack, unpack, upto, packed, near_hot, rest_hot, natural, cache, part2,
    land2, full1, full2, att, acc, acc4, squares, partial, sums_in, outgo, back, local_sem,
    send_sem, recv_sem,
):
    g = lax.axis_index("grp")
    t = lax.axis_index("tp")
    here = Here()
    core = here.core = t % 2
    z = here.z = (t // 2) % RING
    xl = here.xl = t // (2 * RING)
    quarter = core * 2 + xl

    def place(x, zz, cc):
        return (x * RING + zz) * 2 + cc

    here.zp = (g, place(xl, lax.rem(z + 1, RING), core))
    here.zm = (g, place(xl, lax.rem(z + RING - 1, RING), core))
    here.xm = (g, place(1 - xl, z, core))
    here.cp = (g, place(xl, z, 1 - core))
    dg = (g, place(1 - xl, z, 1 - core))
    og = lax.rem(g + GROUPS // 2, GROUPS)
    xm_other = (og, here.xm[1])
    dg_other = (og, dg[1])
    cp_quarter = (1 - core) * 2 + xl
    xm_quarter = core * 2 + (1 - xl)
    dg_quarter = (1 - core) * 2 + (1 - xl)
    mates = [(lax.rem(g + k, GROUPS), t) for k in range(1, GROUPS)]

    def wide(i, n):
        return pl.ds(pl.multiple_of(i * n, n), n)

    def table_half(c):
        return table_ref.at[:, pl.ds(pl.multiple_of(c * CORE_SPAN, CORE_SPAN), CORE_SPAN)]

    table_load = pltpu.make_async_copy(table_half(core), tabs.at[core], local_sem.at[0])
    loads = [
        pltpu.make_async_copy(cache_ref, natural, local_sem.at[6]),
        pltpu.make_async_copy(wq_ref, wqkv.at[:, pl.ds(0, HEAD)], local_sem.at[1]),
        pltpu.make_async_copy(wkv_ref.at[0], wqkv.at[:, pl.ds(HEAD, HEAD)], local_sem.at[2]),
        pltpu.make_async_copy(wkv_ref.at[1], wqkv.at[:, pl.ds(2 * HEAD, HEAD)], local_sem.at[3]),
        pltpu.make_async_copy(wo_ref.at[:, wide(quarter, SPAN)], woq.at[quarter], local_sem.at[4]),
        pltpu.make_async_copy(wp_ref.at[wide(quarter, SPAN)], wpq.at[quarter], local_sem.at[5]),
    ]
    others = [cp_quarter, xm_quarter, dg_quarter]
    stages = [
        pltpu.make_async_copy(wo_ref.at[:, wide(q, SPAN)], staged.at[q], local_sem.at[7 + n])
        for n, q in enumerate(others)
    ]
    table_load.start()
    for copy in stages + loads:
        copy.start()
    info[g] = jnp.full((16, LANES), -1, jnp.int32)
    info[g, 0:4, 0:OWN] = tokens_ref[...]
    info[g, 8:9, 0:OWN] = slots_ref[...].reshape(1, OWN)

    barrier = pltpu.get_barrier_semaphore()
    peers = [here.zp, here.zm, here.xm, here.cp, dg, xm_other, dg_other] + mates
    for peer in peers:
        pl.semaphore_signal(barrier, inc=1, device_id=peer, device_id_type=MESH)
    pl.semaphore_wait(barrier, len(peers))

    wire = Wire(send_sem, recv_sem)
    told = [wire.send(info.at[g], info.at[g], mate) for mate in mates]
    table_in = wire.send(table_half(1 - core), tabs.at[core], here.cp)

    for stage in stages:
        stage.wait()
    receivers = list(zip((here.cp, xm_other, dg_other), others))
    wo_in = [wire.send(staged.at[q], woq.at[quarter], who) for who, q in receivers]
    upto[...] = (
        lax.broadcasted_iota(jnp.int32, (512, 512), 0) <= lax.broadcasted_iota(jnp.int32, (512, 512), 1)
    ).astype(F32).astype(BF)
    for load in loads:
        load.wait()
    for k in range(2):
        for b in range(4):
            rows = slice(b * 80, b * 80 + 80)
            block = natural[k, rows].astype(F32)
            for c in range(CACHE):
                cache[k, c, rows] = block[:, c, :].astype(BF)

    corner = lax.broadcasted_iota(jnp.int32, (WIDE, WIDE), 0) == lax.broadcasted_iota(
        jnp.int32, (WIDE, WIDE), 1
    )

    def fold(f, carry):
        for j in range(4):
            i = j * 8 + f
            gain = jnp.sum(jnp.where(corner, gain_row(gain_ref, i), 0.0), axis=1, keepdims=True)
            folded[wide(f, WIDE), j * QKV : (j + 1) * QKV] = (
                wqkv[wide(i, WIDE), :].astype(F32) * gain
            ).astype(BF)
        return carry

    lax.fori_loop(0, 8, fold, 0)
    for copy in told:
        copy.wait_recv()

    slots = lax.broadcasted_iota(jnp.int32, (OWN, LANES), 0) + g * OWN
    down = jnp.zeros((OWN, 8), F32)
    across = jnp.zeros((8, OWN), F32)
    for e in range(GROUPS):
        hit = (info[e, 8:9, :] == slots).astype(F32).astype(BF)
        member[e] = hit
        heard = info[e, 0:4, :]
        heard = jnp.concatenate([heard >> 7, heard & 127], axis=0).astype(F32).astype(BF)
        down = down + dot_lanes(hit, heard)
        across = across + dot_lanes(heard, hit)
    ids = down[:, 0:4] * 128.0 + down[:, 4:8]
    ids_across = across[0:4] * 128.0 + across[4:8]

    local = (ids - ((xl * RING + z) * (2 * VOCAB_ROWS)).astype(F32)).astype(jnp.int32)
    names = lax.broadcasted_iota(jnp.int32, (OWN, 512), 1)
    seen = []
    for e in range(2):
        hits = jnp.zeros((OWN, 512), F32)
        for j in range(4):
            hits = jnp.where(local[:, j : j + 1] - e * VOCAB_ROWS == names, 1.0, hits)
        seen.append(jnp.where(names[0:1] < VOCAB_ROWS, jnp.max(hits, axis=0, keepdims=True), 0.0))
    ranks = dot(jnp.concatenate(seen, axis=0).astype(BF), upto[...])
    ranks = [ranks[0:1], ranks[1:2] + ranks[0:1, 511:512]]
    order = lax.broadcasted_iota(jnp.int32, (PACK, 512), 0).astype(F32) + 1.0
    picks = [jnp.where(ranks[e] == order, seen[e], 0.0).astype(BF)[:, 0:VOCAB_ROWS] for e in range(2)]

    table_load.wait()
    table_in.wait_recv()
    for e in range(4):
        columns = slice(e * WIDE, (e + 1) * WIDE)
        value = dot(picks[0], tabs[0, :, columns]) + dot(picks[1], tabs[1, :, columns])
        packed[core * 4 + e, 0, xl] = value.astype(BF)

    gxx, gc = {}, {}

    def view(s, d, first=0, n=None):
        side = 1 - xl if s == 2 else xl
        at = core * 4 + (0 if s == 0 else 2) + first
        return packed.at[pl.ds(at, 2 if n is None else n), PLACES[d % RING], side]

    def beyond(s, d):
        ref = view(s, d)
        gxx[d] = wire.send(ref, ref, here.xm)
        gc[s, d] = wire.send(ref, ref, here.cp)

    def beside(s, d):
        ref = view(s, d)
        gc[s, d] = wire.send(ref, ref, here.cp)

    def late(d):
        gxx[d].wait_recv()
        ref = packed.at[pl.ds(core * 4, 2), PLACES[d % RING], 1 - xl]
        gc[3, d] = wire.send(ref, ref, here.cp)

    share = Share(wire, here, view, [(SPLIT, beyond), (SPLIT, beside), (SPLIT, beside)], 1)
    ref = view(1, 0)
    swap = wire.send(ref, ref, here.xm)
    share.begin(0)
    share.begin(1)
    swap.wait_recv()
    share.begin(2)
    for s in range(3):
        share.hop(1, s)
    late(0)

    shares = jnp.floor((ids + 0.5) * (0.5 / VOCAB_ROWS))
    lowest = shares * (2.0 * VOCAB_ROWS)
    earlier = lax.broadcasted_iota(jnp.int32, (OWN, OWN), 0) < lax.broadcasted_iota(
        jnp.int32, (OWN, OWN), 1
    )
    firsts = []
    for j in range(4):
        row = ids_across[j : j + 1]
        again = jnp.where(earlier & (ids[:, j : j + 1] == row), 1.0, 0.0)
        for i in range(j):
            again = jnp.where(ids[:, i : i + 1] == row, 1.0, again)
        firsts.append(jnp.where(jnp.max(again, axis=0, keepdims=True) > 0.0, -1.0, row))
    rank = []
    for j in range(4):
        below = jnp.zeros((OWN, OWN), F32)
        for i in range(4):
            inside = (firsts[i] >= lowest[:, j : j + 1]) & (firsts[i] < ids[:, j : j + 1])
            below = below + jnp.where(inside, 1.0, 0.0)
        rank.append(jnp.sum(below, axis=1, keepdims=True))
    rank = jnp.concatenate(rank, axis=1)
    over = jnp.max(jnp.where(rank >= PACK, 1.0, 0.0))
    column = jnp.where(shares >= RING, 1.0, 0.0)
    apart = shares - column * RING - z.astype(F32)
    apart = jnp.where(apart < 0.0, apart + RING, apart)
    slab = jnp.where(apart < 4.0, 2.0 * apart, jnp.where(apart == 4.0, 7.0, 15.0 - 2.0 * apart))
    spot = (slab * SLAB + column * PACK + rank).astype(jnp.int32)
    for j in range(4):
        near_hot[j] = (
            spot[:, j : j + 1] == lax.broadcasted_iota(jnp.int32, (OWN, NEAR), 1)
        ).astype(F32).astype(BF)
        rest_hot[j] = (
            spot[:, j : j + 1] - NEAR == lax.broadcasted_iota(jnp.int32, (OWN, REST), 1)
        ).astype(F32).astype(BF)

    for s in range(3):
        share.hop(2, s)
    late(-1)
    late(1)

    upper = (
        lax.broadcasted_iota(jnp.int32, (LANES, LANES), 0)
        <= lax.broadcasted_iota(jnp.int32, (LANES, LANES), 1)
    ).astype(F32).astype(BF)
    places = lax.broadcasted_iota(jnp.int32, (CAP, LANES), 0).astype(F32)
    own_slots = info[g, 8:9, :]
    for e in range(GROUPS):
        row = info[e, 8:9, :] - g * OWN
        inside = ((row >= 0) & (row < OWN)).astype(F32)
        rank = dot(inside.astype(BF), upper)
        pick = jnp.where(rank - 1.0 == places, inside, 0.0).astype(BF)
        pack[e] = dot_lanes(pick, member[e]).astype(BF)
        row = own_slots - e * OWN
        inside = ((row >= 0) & (row < OWN)).astype(F32)
        rank = dot(inside.astype(BF), upper)
        unpack[e] = jnp.where(rank - 1.0 == places, inside, 0.0).astype(BF)


    def arrived(*apart):
        for s in range(4):
            for d in apart:
                gc[s, d].wait_recv()

    def multiply(a, b):
        rows = slice(a * SLAB, b * SLAB)
        count = (b - a) * SLAB

        def step(n, carry):
            left = [packed[f, a:b].reshape(count, WIDE) for f in range(8)]
            value = dot(jnp.concatenate(left, axis=1), folded[:, wide(n, WIDE)])
            product[rows, wide(n, WIDE)] = value.astype(BF)
            return carry

        lax.fori_loop(0, 4 * QKV // WIDE, step, 0)
        sq = None
        for f in range(8):
            value = packed[f, a:b].reshape(count, WIDE).astype(F32)
            sq = value * value if sq is None else sq + value * value
        sq = jnp.sum(sq, axis=1, keepdims=True)
        high = sq.astype(BF).astype(F32)
        lanes = lax.broadcasted_iota(jnp.int32, (count, HEAD), 1)
        product[rows, 4 * QKV :] = jnp.where(lanes < HEAD // 2, high, sq - high).astype(BF)

    def pick(hot, rows):
        total = None
        for j in range(4):
            right = [product[rows, j * QKV : (j + 1) * QKV], product[rows, 4 * QKV :]]
            term = dot(hot[j], jnp.concatenate(right, axis=1))
            total = term if total is None else total + term
        return total

    for s in range(3):
        share.hop(3, s)
    late(-2)
    late(2)
    wp_in = [wire.send(wp_ref.at[wide(q, SPAN)], wpq.at[quarter], who) for who, q in receivers]
    arrived(0, -1, 1)
    multiply(0, 3)
    for s in range(3):
        share.hop(4, s)
    late(-3)
    late(3)
    arrived(-2, 2)
    multiply(3, 5)
    late(4)
    arrived(-3, 3)
    multiply(5, 7)
    acc[...] = pick(near_hot, slice(0, NEAR))
    arrived(4)
    multiply(7, 8)
    acc[...] += pick(rest_hot, slice(NEAR, ALL))
    square = acc[:, QKV : QKV + 1] + acc[:, QKV + HEAD // 2 : QKV + HEAD // 2 + 1]
    scale = lax.rsqrt(square * (1.0 / (CHUNKS * WIDE)) + EPSILON)

    queries = (acc[:, 0:HEAD] * scale).astype(BF).astype(F32)
    keys = (acc[:, HEAD : 2 * HEAD] * scale).astype(BF).astype(F32)
    values = (acc[:, 2 * HEAD : QKV] * scale).astype(BF).astype(F32)
    root = 1.0 / HEAD**0.5
    diagonal = lax.broadcasted_iota(jnp.int32, (OWN, OWN), 0) == lax.broadcasted_iota(
        jnp.int32, (OWN, OWN), 1
    )
    lens = jnp.sum(
        jnp.where(diagonal, lens_ref[...].reshape(1, OWN).astype(F32), 0.0), axis=1, keepdims=True
    )
    scores = []
    for c in range(CACHE):
        s = jnp.sum(queries * cache[0, c].astype(F32), axis=1, keepdims=True) * root
        scores.append(jnp.where(lens > c + 0.5, s, -1e30))
    scores.append(jnp.sum(queries * keys, axis=1, keepdims=True) * root)
    top = functools.reduce(jnp.maximum, scores)
    raised = [jnp.exp(s - top) for s in scores]
    whole = functools.reduce(jnp.add, raised)
    weights = [(r / whole).astype(BF).astype(F32) for r in raised]
    mixed = weights[CACHE] * values
    for c in range(CACHE):
        mixed = mixed + weights[c] * cache[1, c].astype(F32)
    att[quarter] = mixed.astype(BF)
    att_in = [wire.send(att.at[quarter], att.at[quarter], who) for who in (here.xm, dg, here.cp)]

    def lay(f, carry):
        full1[f] = (
            dot(near_hot[quarter], packed[f, 0:7].reshape(NEAR, WIDE))
            + dot(rest_hot[quarter], packed[f, 7].reshape(REST, WIDE))
        ).astype(BF)
        return carry

    lax.fori_loop(0, 8, lay, 0)
    for copy in att_in + wo_in:
        copy.wait_recv()

    def spread(i, carry):
        zz = lax.rem(z + ring_order(i), RING)
        both = jnp.concatenate([att[q] for q in range(QUAD)], axis=1)
        blocks = [woq[q, :, wide(zz, WIDE)] for q in range(QUAD)]
        part2[zz] = dot(both, jnp.concatenate(blocks, axis=0)).astype(BF)
        return carry

    strips = [(lambda zz: zz, QUART * s, QUART, (UP, DOWN)[s % 2], None) for s in range(QUAD)]
    ring = Ring(wire, here, part2, land2, strips)
    spread(0, 0)
    for s in range(QUAD):
        ring.hop0(s)
    lax.fori_loop(1, RING, spread, 0)
    for k in (1, 2, 3):
        for s in range(QUAD):
            ring.hop(k, s)

    def strip(s, d, first=0, n=QUART):
        return full2.at[ring.zat(d), pl.ds(QUART * s + first, n)]

    share = Share(
        wire, here, lambda s, d, a, n: strip(s, d, 0, QUART), [(far, None) for _, _, _, far, _ in strips], 0
    )
    for s in range(QUAD):
        rows = slice(QUART * s, QUART * s + QUART)
        value = ring.total(s) + full1[z, rows].astype(F32)
        full2[z, rows] = value.astype(BF)
        share.begin(s)

    def take(zz, first):
        value = full2[zz].astype(F32)
        scaled = (value * gain_row(final_ref, quarter * RING + zz)).astype(BF)
        blocks = [wpq[q, wide(zz, WIDE), :] for q in range(QUAD)]
        term = dot(scaled, jnp.concatenate(blocks, axis=1))
        if first:
            acc4[...] = term
            squares[...] = value * value
        else:
            acc4[...] += term
            squares[...] += value * value

    for copy in wp_in:
        copy.wait_recv()
    take(z, True)
    for k in (1, 2, 3, 4):
        for s in range(QUAD):
            share.hop(k, s)
        take(ring.zat(-k), False)
        if k < 4:
            take(ring.zat(k), False)

    for q in range(QUAD):
        partial[q] = acc4[:, q * HEAD : (q + 1) * HEAD].astype(BF)
    mine = [
        wire.send(partial.at[q], back.at[quarter], who)
        for who, q in ((here.xm, xm_quarter), (dg, dg_quarter), (here.cp, cp_quarter))
    ]
    square = lax.dot_general(
        jnp.ones((8, WIDE), F32),
        squares[...],
        (((1,), (1,)), ((), ())),
        preferred_element_type=F32,
        precision=lax.Precision.HIGHEST,
    )
    sums_in[quarter] = square
    mine += [
        wire.send(sums_in.at[quarter], sums_in.at[quarter], who) for who in (here.xm, dg, here.cp)
    ]
    back[quarter] = partial[quarter]
    for copy in mine:
        copy.wait_recv()
    prefix, square = None, None
    for q in range(QUAD):
        term = back[q].astype(F32)
        prefix = term if prefix is None else prefix + term
        square = sums_in[q, 0:1] if square is None else square + sums_in[q, 0:1]
    square = lax.rsqrt(square * (1.0 / (CHUNKS * WIDE)) + EPSILON)
    square = jnp.sum(jnp.where(diagonal, square, 0.0), axis=1, keepdims=True)
    prefix = (prefix * square).astype(BF)
    homes = []
    away = CAP + FLAG
    for e in range(GROUPS):
        outgo[e, CAP:away] = jnp.full((FLAG, HEAD), over, F32).astype(BF)
    for k, mate in enumerate(mates):
        outgo[mate[0], 0:CAP] = dot(pack[mate[0]], prefix).astype(BF)
        homes.append(wire.send(outgo.at[mate[0], pl.ds(0, away)], outgo.at[g, pl.ds(away, away)], mate))
    outgo[g, away : away + CAP] = dot(pack[g], prefix).astype(BF)
    outgo[g, away + CAP : 2 * away] = jnp.full((FLAG, HEAD), over, F32).astype(BF)
    for copy in homes:
        copy.wait_recv()
    result = jnp.zeros((LANES, HEAD), F32)
    flag = jnp.zeros((FLAG, HEAD), F32)
    for e in range(GROUPS):
        flag = jnp.maximum(flag, outgo[e, away + CAP : 2 * away].astype(F32))
        result = result + lax.dot_general(
            unpack[e], outgo[e, away : away + CAP], (((0,), (0,)), ((), ())), preferred_element_type=F32
        )
    out_ref[...] = result[0:OWN].astype(BF)
    flag_ref[0, 0] = jnp.max(flag).astype(jnp.int32)
    for copy in wire.sent:
        copy.wait_send()


def sum_shares(rows):
    count = lax.axis_size("tp")
    blocks = rows.reshape(rows.shape[0], count, -1).transpose(1, 0, 2)
    blocks = lax.all_to_all(blocks, "tp", split_axis=0, concat_axis=0, tiled=True)
    return jnp.sum(blocks.astype(jnp.float32), axis=0)


def all_shares(rows):
    count = lax.axis_size("tp")
    blocks = jnp.broadcast_to(rows[None], (count,) + rows.shape)
    blocks = lax.all_to_all(blocks, "tp", split_axis=0, concat_axis=0, tiled=True)
    return blocks.transpose(1, 0, 2).reshape(rows.shape[0], -1)


def rms_scale(rows, gain):
    values = rows.astype(jnp.float32)
    spread = jnp.mean(values * values, axis=-1, keepdims=True)
    return (values * lax.rsqrt(spread + EPSILON) * gain).astype(jnp.bfloat16)


def routing(slot_ids, owned, groups, capacity):
    target = slot_ids // owned
    place_in = slot_ids % owned
    member = (target[:, None] == jnp.arange(groups, dtype=jnp.int32)[None, :]).astype(jnp.int32)
    within = jnp.sum((jnp.cumsum(member, axis=0) - 1) * member, axis=1)
    return (target * capacity + within, place_in)


def pack_rows(values, slot_index, total):
    buffer = jnp.zeros((total,) + values.shape[1:], values.dtype)
    return buffer.at[slot_index].set(values)


def lookup_part(token_ids, table):
    vocab_rows = table.shape[0]
    local_ids = token_ids - lax.axis_index("tp") * vocab_rows
    inside = (local_ids >= 0) & (local_ids < vocab_rows)
    picked = jnp.take(table, jnp.clip(local_ids, 0, vocab_rows - 1), axis=0)
    picked = jnp.where(inside[..., None], picked, jnp.zeros_like(picked))
    return picked.reshape(token_ids.shape[0], -1).astype(jnp.float32)


def attend(normed, query_weight, key_value_weight, kv_cache, cache_lengths):
    row_count = normed.shape[0]
    queries = jnp.dot(normed, query_weight, preferred_element_type=jnp.float32).astype(jnp.bfloat16)
    fresh = jnp.einsum(
        "rg,kgd->krd", normed, key_value_weight, preferred_element_type=jnp.float32
    ).astype(jnp.bfloat16)
    heads_here = queries.shape[1] // HEAD
    query_heads = queries.reshape(row_count, heads_here, HEAD)
    key_heads = fresh[0].reshape(row_count, heads_here, HEAD)
    value_heads = fresh[1].reshape(row_count, heads_here, HEAD)
    cached = kv_cache.reshape(2, row_count, CACHE, heads_here, HEAD)
    scale = 1.0 / HEAD**0.5
    past = (
        jnp.einsum("rhd,rchd->rhc", query_heads, cached[0], preferred_element_type=jnp.float32)
        * scale
    )
    valid = jnp.arange(CACHE, dtype=jnp.int32)[None, None, :] < cache_lengths[:, None, None]
    past = jnp.where(valid, past, jnp.float32(-1e30))
    own_score = (
        jnp.sum(query_heads.astype(jnp.float32) * key_heads.astype(jnp.float32), axis=-1)[..., None]
        * scale
    )
    weights = jax.nn.softmax(jnp.concatenate([past, own_score], axis=-1), axis=-1).astype(
        jnp.bfloat16
    )
    mixed = jnp.einsum(
        "rhc,rchd->rhd", weights[..., :-1], cached[1], preferred_element_type=jnp.float32
    )
    mixed = mixed + weights[..., -1:].astype(jnp.float32) * value_heads.astype(jnp.float32)
    return mixed.reshape(row_count, -1).astype(jnp.bfloat16)


def plain(
    block_tokens,
    slot_of_row,
    cache_lengths,
    embed_table,
    norm_gain,
    query_weight,
    key_value_weight,
    kv_cache,
    out_weight,
    final_gain,
    prefix_weight,
):
    groups = lax.axis_size("grp")
    owned = slot_of_row.shape[0]
    capacity = 2 * owned // groups
    total = groups * capacity
    slot_index, place_in = routing(slot_of_row, owned, groups, capacity)
    sent_place = (
        jnp.full((total,), owned, jnp.int32).at[slot_index].set(place_in).reshape(groups, capacity)
    )
    shares = sum_shares(lookup_part(block_tokens, embed_table).astype(jnp.bfloat16)).astype(jnp.bfloat16)
    sent_rows = pack_rows(shares, slot_index, total).reshape(groups, capacity, -1)
    got_rows, got_place = (
        lax.all_to_all(sent_rows, "grp", split_axis=0, concat_axis=0, tiled=True),
        lax.all_to_all(sent_place, "grp", split_axis=0, concat_axis=0, tiled=True),
    )
    got_place = got_place.reshape(total)
    own_part = (
        jnp.zeros((owned, shares.shape[1]), jnp.bfloat16)
        .at[got_place]
        .set(got_rows.reshape(total, -1), mode="drop")
    )
    whole = all_shares(own_part)
    normed = rms_scale(whole, norm_gain)
    attended = attend(normed, query_weight, key_value_weight, kv_cache, cache_lengths)
    partial_value = jnp.dot(attended, out_weight, preferred_element_type=jnp.float32)
    summed = sum_shares(partial_value.astype(jnp.bfloat16))
    context = (own_part.astype(jnp.float32) + summed).astype(jnp.bfloat16)
    source_rows = jnp.minimum(got_place, owned - 1)
    back_rows = jnp.take(context, source_rows, axis=0).reshape(groups, capacity, -1)
    home_rows = lax.all_to_all(back_rows, "grp", split_axis=0, concat_axis=0, tiled=True).reshape(
        total, -1
    )
    mine = jnp.take(home_rows, slot_index, axis=0)
    full_rows = all_shares(mine)
    return jnp.dot(
        rms_scale(full_rows, final_gain), prefix_weight, preferred_element_type=jnp.float32
    ).astype(jnp.bfloat16)


def shards(
    block_tokens, slot_of_row, cache_lengths, embed_table, norm_gain, query_weight, key_value_weight,
    kv_cache, out_weight, final_gain, prefix_weight,
):
    vmem = pl.BlockSpec(memory_space=pltpu.VMEM)
    hbm = pl.BlockSpec(memory_space=pl.ANY)
    out, flag = pl.pallas_call(
        kernel,
        out_shape=[jax.ShapeDtypeStruct((OWN, HEAD), BF), jax.ShapeDtypeStruct((1, 1), jnp.int32)],
        in_specs=[vmem] * 5 + [hbm] * 6,
        out_specs=[vmem, pl.BlockSpec(memory_space=pltpu.SMEM)],
        scratch_shapes=[
            pltpu.VMEM((GROUPS, 16, LANES), jnp.int32),
            pltpu.VMEM((2, VOCAB_ROWS, CORE_SPAN), BF),
            pltpu.VMEM((CHUNKS * WIDE, 3 * HEAD), BF),
            pltpu.VMEM((SPAN, 4 * QKV), BF),
            pltpu.VMEM((ALL, 4 * QKV + HEAD), BF),
            pltpu.VMEM((QUAD, HEAD, SPAN), BF),
            pltpu.VMEM((QUAD, HEAD, SPAN), BF),
            pltpu.VMEM((QUAD, SPAN, HEAD), BF),
            pltpu.VMEM((GROUPS, OWN, LANES), BF),
            pltpu.VMEM((GROUPS, CAP, OWN), BF),
            pltpu.VMEM((GROUPS, CAP, LANES), BF),
            pltpu.VMEM((512, 512), BF),
            pltpu.VMEM((8, RING, 2, PACK, WIDE), BF),
            pltpu.VMEM((4, OWN, NEAR), BF),
            pltpu.VMEM((4, OWN, REST), BF),
            pltpu.VMEM((2, OWN, CACHE, HEAD), BF),
            pltpu.VMEM((2, CACHE, OWN, HEAD), BF),
            pltpu.VMEM((RING, OWN, WIDE), BF),
            pltpu.VMEM((QUAD, 2, 4, QUART, WIDE), BF),
            pltpu.VMEM((RING, OWN, WIDE), BF),
            pltpu.VMEM((RING, OWN, WIDE), BF),
            pltpu.VMEM((QUAD, OWN, HEAD), BF),
            pltpu.VMEM((OWN, QUAD * HEAD), F32),
            pltpu.VMEM((OWN, QUAD * HEAD), F32),
            pltpu.VMEM((OWN, WIDE), F32),
            pltpu.VMEM((QUAD, OWN, HEAD), BF),
            pltpu.VMEM((QUAD, 8, OWN), F32),
            pltpu.VMEM((GROUPS, 2 * (CAP + FLAG), HEAD), BF),
            pltpu.VMEM((QUAD, OWN, HEAD), BF),
            pltpu.SemaphoreType.DMA((10,)),
            pltpu.SemaphoreType.DMA((SEMS,)),
            pltpu.SemaphoreType.DMA((SEMS,)),
        ],
        compiler_params=pltpu.CompilerParams(
            collective_id=0, has_side_effects=True, vmem_limit_bytes=60 * 1024 * 1024
        ),
    )(
        block_tokens.T,
        slot_of_row,
        cache_lengths,
        norm_gain.reshape(2 * CHUNKS, HEAD),
        final_gain.reshape(2 * CHUNKS, HEAD),
        kv_cache,
        embed_table,
        query_weight,
        key_value_weight,
        out_weight,
        prefix_weight,
    )
    return lax.cond(
        flag[0, 0] > 0,
        lambda: plain(
            block_tokens, slot_of_row, cache_lengths, embed_table, norm_gain, query_weight,
            key_value_weight, kv_cache, out_weight, final_gain, prefix_weight,
        ),
        lambda: out,
    )


def solution(mesh):
    in_specs = (
        P("grp", None),
        P("grp"),
        P("grp"),
        P("tp", None),
        P(),
        P(None, "tp"),
        P(None, None, "tp"),
        P(None, "grp", None, "tp"),
        P("tp", None),
        P(),
        P(None, "tp"),
    )
    return jax.shard_map(
        shards, mesh=mesh, in_specs=in_specs, out_specs=P("grp", "tp"), check_vma=False
    )
```
